32 devices in a mesh: groups: 2 (over x), mesh: 16 (over z, y, core).
Axes of the slice: x: 2, y: 2, z: 4, core: 2. Of those that a mesh axis runs over, the one named last changes fastest.
Arguments:
- mesh_state: bfloat16 [128, 128, 512], P(('groups', 'mesh')), parts along dimension 0, may hold values from -8 to 8
- obs_latent: bfloat16 [1024, 128, 512], P(('groups', 'mesh')), parts along dimension 0, may hold values from -6 to 6
- pair_coupling: bfloat16 [1024, 128, 128], P(('groups', 'mesh')), parts along dimension 0, may hold values from -0.5 to 0.5
- pair_target: int32 [1024], P(('groups', 'mesh')), parts along dimension 0, may hold values from 0 to 11
- pair_source: int32 [1024], P(('groups', 'mesh')), parts along dimension 0, may hold values from 0 to 31
- pair_count: int32 [32], P(('groups', 'mesh')), parts along dimension 0, may hold values from 1 to 32, 256 in all
- mesh_coupling: bfloat16 [64, 4, 128, 128], P('mesh'), may hold values from -0.25 to 0.25
- neighbor: int32 [64, 4], P('mesh'), may hold values from 0 to 5, as said below
- rim_send: int32 [16, 2], P('mesh'), may hold values from 0 to 3, as said below
- enc_gain: float32 [512], replicated, may hold values from 0.25 to 1.75
- enc_self: bfloat16 [512, 512], replicated, may hold values from -0.25 to 0.25
- enc_obs: bfloat16 [512, 512], replicated, may hold values from -0.25 to 0.25
- enc_out: bfloat16 [512, 512], replicated, may hold values from -0.25 to 0.25
- node_gain: float32 [2, 512], replicated, may hold values from 0.25 to 1.75
- node_self: bfloat16 [2, 512, 512], replicated, may hold values from -0.25 to 0.25
- node_msg: bfloat16 [2, 512, 512], replicated, may hold values from -0.25 to 0.25
- node_out: bfloat16 [2, 512, 512], replicated, may hold values from -0.25 to 0.25
Outputs:
- mesh_out: bfloat16 [128, 128, 512], P(('groups', 'mesh')), parts along dimension 0
The draws below stay inside these ranges and needn't reach their ends.
There are 2 independent parts, one for each index of `groups`. The reference program is written for one: setup_inputs(seed, part) draws one part's arguments, and reference() takes and returns one part's arrays. A program takes and returns all parts, laid end to end along the dimension named above; an argument that names none is the same for every part. Nothing has to cross between parts.
Inputs may be any that keep to these rules, and one draw needn't show every extreme that they name: pair_target // 4 - 1 is the offset (-1, 0 or 1) along mesh, modulo 16, from the pair's device to the device that owns the fed block; pair_target mod 4 is that block's local index there. `pair_source`: local observation block on the pair's own device. A device's live pairs are its first pair_count slots; some device has all 32 live. `neighbor`: values index a device's receive list: 0 the block from the left neighbour, 1 + c the local block c, 5 the block from the right neighbour; the entry at position 0 of each row is the block itself, the entry at position 1 lies before it in this list, the entry at position 2 after it. `rim_send`: two different local blocks of each device: the one sent to the left neighbour, then the one sent to the right.
All inputs are finite; a program needn't handle non-finite values.
Results may differ from the reference program's by a relative error of at most 0.014.
Values may be sent and summed in bfloat16 or wider, within the bound.
No kernel may reach another device: no remote copies, remote signals or barrier semaphores. Data moves between devices by JAX's collectives and lax.ppermute only.
A program may use at most 128 MiB of HBM per device.

```python
import math
import jax
import jax.numpy as jnp
import numpy as np
from jax import lax

D = 512
BLK = 128
K_ADJ = 4
ROUNDS = 2
MB_DEV = 4
OB_DEV = 32
PAIR_DEV = 32
PEERS = 16
MESH_BLOCKS = 64
OBS_BLOCKS = 512
PAIRS = 512


def draw_mesh_state(key, part):
    key = jax.random.fold_in(key, 11)
    key_base = jax.random.fold_in(key, 0)
    values = jax.random.normal(key_base, (MESH_BLOCKS, BLK, D), jnp.float32)
    return jnp.clip(values, -8.0, 8.0).astype(jnp.bfloat16)


def draw_neighbor(key, part):
    key = jax.random.fold_in(key, 12)
    key_below, key_above, key_any = jax.random.split(key, 3)
    local_index = jnp.arange(MESH_BLOCKS, dtype=jnp.int32) % MB_DEV
    itself = local_index + 1
    below = jax.random.randint(key_below, (MESH_BLOCKS,), 0, itself, dtype=jnp.int32)
    above = jax.random.randint(key_above, (MESH_BLOCKS,), itself + 1, MB_DEV + 2, dtype=jnp.int32)
    anywhere = jax.random.randint(key_any, (MESH_BLOCKS,), 0, MB_DEV + 2, dtype=jnp.int32)
    return jnp.stack([itself, below, above, anywhere], axis=1).astype(jnp.int32)


def draw_rim_send(key, part):
    key = jax.random.fold_in(key, 13)
    scores = jax.random.randint(key, (PEERS, MB_DEV), 0, 1 << 20, dtype=jnp.int32) * MB_DEV
    scores = scores + jnp.arange(MB_DEV, dtype=jnp.int32)[None, :]
    ordering = jnp.argsort(scores, axis=1)
    return ordering[:, :2].astype(jnp.int32)


def touch_ends(result, rng, least, high):
    dims = result.shape
    spot = [jax.random.randint(jax.random.fold_in(rng, axis), (), 0, dims[axis]) for axis in range(len(dims))]
    result = result.at[tuple(spot)].set(least)
    longest = dims.index(max(dims))
    spot[longest] = (spot[longest] + 1) % dims[longest]
    return result.at[tuple(spot)].set(high)


def shard_levels(rng, shape, cuts, smallest, largest):
    gain = 1.0
    for dim, blocks in cuts:
        draws = jax.random.uniform(jax.random.fold_in(jax.random.fold_in(rng, 6), dim), (blocks,), jnp.float32, smallest / len(cuts), largest / len(cuts))
        gain = gain * jnp.repeat(jnp.exp(draws), shape[dim] // blocks).reshape((-1,) + (1,) * (len(shape) - 1 - dim))
    return gain


def length_profile(number_of, total, bound, skew):
    portions = [(1 << 20) // math.isqrt(rank ** skew) + 1 for rank in range(2, number_of + 1)]
    rest, counts = total - bound - (number_of - 1), [1] * (number_of - 1)
    while rest > 0:
        free = [i for i in range(number_of - 1) if counts[i] < bound]
        pool, left = sum([portions[i] for i in free]), rest
        for i in free:
            more = min(bound - counts[i], max(1, left * portions[i] // pool), rest)
            counts[i] = counts[i] + more
            rest = rest - more
    return np.array([bound] + counts)


def ragged(own_key, amount, total, limit, slope):
    if amount == 2:
        one = jax.random.randint(own_key, (), max(1, total - limit), min(limit, total - 1) + 1)
        return jnp.stack([one, total - one])
    lengths = jnp.asarray(length_profile(amount, total, limit, slope), jnp.int32)
    pairs = (amount - 1) // 2
    giver, taker = lengths[1:1 + 2 * pairs:2], lengths[2:2 + 2 * pairs:2]
    room = jnp.minimum(giver - 1, limit - taker)
    passed = jax.random.randint(jax.random.fold_in(own_key, 1), (pairs,), 0, 1 << 20) % (room + 1)
    lengths = lengths.at[1:1 + 2 * pairs:2].set(giver - passed).at[2:2 + 2 * pairs:2].set(taker + passed)
    return lengths[jax.random.permutation(jax.random.fold_in(own_key, 2), amount)]


def gaussian(rng, shape, width, limit, cuts=(), kind=jnp.bfloat16):
    array = width * jax.random.normal(rng, shape, jnp.float32)
    if cuts:
        array = array * shard_levels(rng, shape, cuts, -0.22, 0.18)
    return jnp.clip(array, -limit, limit).astype(kind)


def setup_inputs(seed: int = 0, part: int = 0) -> dict:
    key_list = jax.random.split(jax.random.key(seed), 18)
    part_splits = jax.random.split(jax.random.fold_in(key_list[17], part), 18)
    return {
        "mesh_state": draw_mesh_state(jax.random.fold_in(jax.random.fold_in(key_list[17], part), 71), part),
        "obs_latent": gaussian(part_splits[1], (OBS_BLOCKS, BLK, D), 1.0, 6.0, ((0, 16),)),
        "pair_coupling": gaussian(part_splits[2], (PAIRS, BLK, BLK), BLK ** -0.5, 0.5, ((0, 16),)),
        "pair_target": touch_ends(jax.random.randint(part_splits[3], (PAIRS,), 0, 3 * MB_DEV), jax.random.fold_in(part_splits[3], 1), 0, (3 * MB_DEV) - 1).astype(jnp.int32),
        "pair_source": touch_ends(jax.random.randint(part_splits[4], (PAIRS,), 0, OB_DEV), jax.random.fold_in(part_splits[4], 1), 0, OB_DEV - 1).astype(jnp.int32),
        "pair_count": ragged(part_splits[5], PEERS, PEERS * PAIR_DEV // 2, PAIR_DEV, 2).astype(jnp.int32),
        "mesh_coupling": gaussian(key_list[6], (MESH_BLOCKS, K_ADJ, BLK, BLK), (BLK * K_ADJ) ** -0.5, 0.25, ((0, 16),)),
        "neighbor": draw_neighbor(jax.random.fold_in(key_list[17], 71), part),
        "rim_send": draw_rim_send(jax.random.fold_in(key_list[17], 71), part),
        "enc_gain": jnp.clip(1.0 + 0.15 * jax.random.normal(key_list[9], (D,), jnp.float32), 0.25, 1.75),
        "enc_self": gaussian(key_list[10], (D, D), D ** -0.5, 0.25),
        "enc_obs": gaussian(key_list[11], (D, D), D ** -0.5, 0.25),
        "enc_out": gaussian(key_list[12], (D, D), D ** -0.5, 0.25),
        "node_gain": jnp.clip(1.0 + 0.15 * jax.random.normal(key_list[13], (ROUNDS, D), jnp.float32), 0.25, 1.75),
        "node_self": gaussian(key_list[14], (ROUNDS, D, D), D ** -0.5, 0.25),
        "node_msg": gaussian(key_list[15], (ROUNDS, D, D), D ** -0.5, 0.25),
        "node_out": gaussian(key_list[16], (ROUNDS, D, D), D ** -0.5, 0.25),
    }


def layer_norm(values, scale_row):
    values = values.astype(jnp.float32)
    center = values - lax.optimization_barrier(jnp.mean(values, axis=-1, keepdims=True))
    spread = lax.optimization_barrier(jnp.mean(center * center, axis=-1, keepdims=True))
    return center * lax.rsqrt(spread + 1e-05) * scale_row

def node_update(current, normed, incoming, w_first, w_second, w_last):
    flat_norm = normed.reshape(-1, D)
    flat_in = incoming.reshape(-1, D)
    before = jnp.dot(flat_norm, w_first, preferred_element_type=jnp.float32)
    before = before + jnp.dot(flat_in, w_second, preferred_element_type=jnp.float32)
    hidden = jax.nn.silu(before).astype(jnp.bfloat16)
    updated = current.reshape(-1, D).astype(jnp.float32) + jnp.dot(hidden, w_last, preferred_element_type=jnp.float32)
    return updated.astype(jnp.bfloat16).reshape(current.shape)

def reference(mesh_state, obs_latent, pair_coupling, pair_target, pair_source, pair_count, mesh_coupling, neighbor, rim_send, enc_gain, enc_self, enc_obs, enc_out, node_gain, node_self, node_msg, node_out):

    def add_device(total, inputs):
        coupling, targets, sources, count, device = inputs
        chosen = obs_latent[device * OB_DEV + sources]
        products = jnp.einsum('nij,njd->nid', coupling.astype(jnp.float32), chosen.astype(jnp.float32))
        alive = jnp.arange(PAIR_DEV, dtype=jnp.int32) < count
        products = jnp.where(alive[:, None, None], products, jnp.zeros_like(products))
        dest = (device + targets // MB_DEV - 1) % PEERS * MB_DEV + targets % MB_DEV
        return (total.at[dest.astype(jnp.int32)].add(products), None)
    initial = jnp.zeros((MESH_BLOCKS, BLK, D), jnp.float32)
    scanned = (pair_coupling.reshape(PEERS, PAIR_DEV, BLK, BLK), pair_target.reshape(PEERS, PAIR_DEV), pair_source.reshape(PEERS, PAIR_DEV), pair_count, jnp.arange(PEERS, dtype=jnp.int32))
    enc_sum, _ = lax.scan(add_device, initial, scanned)
    enc_in = enc_sum.astype(jnp.bfloat16)
    normed = layer_norm(mesh_state, enc_gain).astype(jnp.bfloat16)
    current = node_update(mesh_state, normed, enc_in, enc_self, enc_obs, enc_out)
    block_ids = jnp.arange(MESH_BLOCKS, dtype=jnp.int32)
    owner = block_ids // MB_DEV
    left_dev = (owner - 1) % PEERS
    right_dev = (owner + 1) % PEERS
    from_left = left_dev * MB_DEV + rim_send[left_dev, 1]
    from_right = right_dev * MB_DEV + rim_send[right_dev, 0]
    inner = owner[:, None] * MB_DEV + neighbor - 1
    global_nbr = jnp.where(neighbor == 0, from_left[:, None], jnp.where(neighbor == MB_DEV + 1, from_right[:, None], inner)).astype(jnp.int32)
    for round_index in range(ROUNDS):
        normed = layer_norm(current, node_gain[round_index]).astype(jnp.bfloat16)

        def device_message(inputs):
            coupling, indices = inputs
            gathered = normed[indices]
            return jnp.einsum('bkij,bkjd->bid', coupling.astype(jnp.float32), gathered.astype(jnp.float32))
        message = lax.map(device_message, (mesh_coupling.reshape(PEERS, MB_DEV, K_ADJ, BLK, BLK), global_nbr.reshape(PEERS, MB_DEV, K_ADJ)))
        message = message.reshape(MESH_BLOCKS, BLK, D).astype(jnp.bfloat16)
        current = node_update(current, normed, message, node_self[round_index], node_msg[round_index], node_out[round_index])
    return current
```

```python
import jax
import jax.numpy as jnp
from jax import lax
from jax.experimental import pallas as pl
from jax.experimental.pallas import tpu as pltpu
from jax.sharding import PartitionSpec as P

F32 = jnp.float32
BF16 = jnp.bfloat16
VMEM = pl.BlockSpec(memory_space=pltpu.VMEM)
SMEM = pl.BlockSpec(memory_space=pltpu.SMEM)
ANY = pl.BlockSpec(memory_space=pl.ANY)


def dot(a, b):
    return jnp.dot(a, b, preferred_element_type=F32)


def silu(v):
    half = 0.5 * v
    return half + half * jnp.tanh(half)


def norm_rows(values, gain):
    center = values - jnp.mean(values, axis=-1, keepdims=True)
    spread = jnp.mean(center * center, axis=-1, keepdims=True)
    return (center * lax.rsqrt(spread + 1e-05) * gain).astype(BF16)


def odd_device():
    return lax.rem(lax.axis_index("mesh"), 2)


def block_order(rim):
    odd = odd_device()
    off = rim[0, odd]
    on = rim[0, 1 - odd]
    low = jnp.minimum(off, on)
    high = jnp.maximum(off, on)
    third = jnp.where(low > 0, 0, jnp.where(high > 1, 1, 2))
    fourth = jnp.where(high < 3, 3, jnp.where(low < 2, 2, 1))
    return [off, on, third, fourth]


def pair_kernel(side, tgt, src, cnt, obs, cpl, out, xbuf, cbuf, acc, xsem, csem):
    blocks = out.shape[0]
    odd = odd_device()
    part = {"off": 2 * odd, "on": 2 - 2 * odd, "self": 1}[side]
    live = cnt[0]

    def local(e):
        t = tgt[e] - part * blocks
        return t, (t >= 0) & (t < blocks)

    def count(e, word):
        t, mine = local(e)
        return word + jnp.where(mine, 1 << (8 * jnp.clip(t, 0, blocks - 1)), 0)

    word = lax.fori_loop(0, live, count, jnp.int32(0))
    counts = [(word >> (8 * t)) & 255 for t in range(blocks)]
    firsts, place = [], jnp.int32(0)
    total = jnp.int32(0)
    for t in range(blocks):
        firsts.append(total)
        place = place + (total << (8 * t))
        total = total + counts[t]

    def fetch(e, place):
        t, mine = local(e)
        shift = 8 * jnp.clip(t, 0, blocks - 1)

        @pl.when(mine)
        def _():
            slot = (place >> shift) & 255
            pltpu.make_async_copy(obs.at[src[e]], xbuf.at[slot], xsem.at[slot]).start()
            pltpu.make_async_copy(cpl.at[e], cbuf.at[slot], csem.at[slot]).start()

        return place + jnp.where(mine, 1 << shift, 0)

    lax.fori_loop(0, live, fetch, place)

    def arrive(slot):
        pltpu.make_async_copy(obs.at[0], xbuf.at[slot], xsem.at[slot]).wait()
        pltpu.make_async_copy(cpl.at[0], cbuf.at[slot], csem.at[slot]).wait()

    for t in range(blocks):
        acc[...] = jnp.zeros_like(acc)

        def two(j, carry):
            slot = firsts[t] + 2 * j
            arrive(slot)
            arrive(slot + 1)
            left = jnp.concatenate([cbuf[slot], cbuf[slot + 1]], axis=1)
            right = jnp.concatenate([xbuf[slot], xbuf[slot + 1]], axis=0)
            acc[...] += dot(left, right)
            return carry

        lax.fori_loop(0, counts[t] // 2, two, 0)

        @pl.when(counts[t] % 2 == 1)
        def _():
            slot = firsts[t] + counts[t] - 1
            arrive(slot)
            acc[...] += dot(cbuf[slot], xbuf[slot])

        out[t] = acc[...].astype(out.dtype)


def pair_sums(side, dtype, blocks, tgt, src, cnt, obs, cpl):
    slots, rows, width = tgt.shape[0], obs.shape[1], obs.shape[2]
    return pl.pallas_call(
        lambda *refs: pair_kernel(side, *refs),
        out_shape=jax.ShapeDtypeStruct((blocks, rows, width), dtype),
        in_specs=[SMEM, SMEM, SMEM, ANY, ANY],
        out_specs=VMEM,
        scratch_shapes=[
            pltpu.VMEM((slots, rows, width), BF16),
            pltpu.VMEM((slots, rows, rows), BF16),
            pltpu.VMEM((rows, width), F32),
            pltpu.SemaphoreType.DMA((slots,)),
            pltpu.SemaphoreType.DMA((slots,)),
        ],
        compiler_params=pltpu.CompilerParams(vmem_limit_bytes=12 << 20),
        cost_estimate=pl.CostEstimate(flops=10 * 2 * 128 * 128 * 512, bytes_accessed=4 << 20, transcendentals=0),
        name="pairs_" + side,
    )(tgt, src, cnt, obs, cpl)


def call(kernel, out, *args, specs=None, flops=0, moved=1 << 20, name=None):
    return pl.pallas_call(
        kernel,
        out_shape=out,
        in_specs=specs or [VMEM] * len(args),
        out_specs=jax.tree.map(lambda _: VMEM, out),
        compiler_params=pltpu.CompilerParams(vmem_limit_bytes=14 << 20),
        cost_estimate=pl.CostEstimate(flops=flops, bytes_accessed=moved, transcendentals=0),
        name=name,
    )(*args)


def prepare_kernel(rim, nbr, state, gain, w_self, coupling, pre, state_p, mix):
    blocks, rows = state.shape[0], state.shape[1]
    order = block_order(rim)
    odd = odd_device()
    last = blocks + 1
    codes = [1 + o for o in order] + [last * odd, last - last * odd]
    for i, m in enumerate(order):
        cut = pl.ds(i * rows, rows)
        values = state[m]
        state_p[cut, :] = values
        pre[cut, :] = dot(norm_rows(values.astype(F32), gain[...]), w_self[...])
        for c, code in enumerate(codes):
            total = None
            for k in range(coupling.shape[1]):
                term = jnp.where(nbr[m, k] == code, coupling[m, k].astype(F32), 0.0)
                total = term if total is None else total + term
            mix[cut, c * rows : (c + 1) * rows] = total.astype(BF16)


def encode_kernel(rim, pre, state_p, own, on, off, w_obs, w_out, gain, state, normed):
    rows = own.shape[1]
    for i, m in enumerate(block_order(rim)):
        cut = pl.ds(i * rows, rows)
        summed = (own[m] + on[m].astype(F32) + off[m].astype(F32)).astype(BF16)
        hidden = silu(pre[cut, :] + dot(summed, w_obs[...])).astype(BF16)
        updated = (state_p[cut, :].astype(F32) + dot(hidden, w_out[...])).astype(BF16)
        state[cut, :] = updated
        normed[cut, :] = norm_rows(updated.astype(F32), gain[...])


def local_kernel(normed, w_self, mix, pre, message):
    size = normed.shape[0]
    pre[...] = dot(normed[...], w_self[...])
    message[...] = dot(mix[:, :size], normed[...])


def round_kernel(last, rim, pre, message, mix, off, on, state, w_msg, w_out, gain, *outs):
    size = state.shape[0]
    rows = off.shape[0]
    rims = jnp.concatenate([off[...], on[...]], axis=0)
    for i, m in enumerate(block_order(rim)):
        cut = pl.ds(i * rows, rows)
        incoming = (message[cut, :] + dot(mix[cut, size:], rims)).astype(BF16)
        hidden = silu(pre[cut, :] + dot(incoming, w_msg[...])).astype(BF16)
        updated = (state[cut, :].astype(F32) + dot(hidden, w_out[...])).astype(BF16)
        if last:
            outs[0][m] = updated
        else:
            outs[0][cut, :] = updated
            outs[1][cut, :] = norm_rows(updated.astype(F32), gain[...])


def shards(
    mesh_state,
    obs_latent,
    pair_coupling,
    pair_target,
    pair_source,
    pair_count,
    mesh_coupling,
    neighbor,
    rim_send,
    enc_gain,
    enc_self,
    enc_obs,
    enc_out,
    node_gain,
    node_self,
    node_msg,
    node_out,
):
    blocks, rows, width = mesh_state.shape
    size = blocks * rows
    count = lax.axis_size("mesh")
    on_route = [(i, i ^ 1) for i in range(count)]
    off_route = [(i, (i + 1) % count if i % 2 else (i - 1) % count) for i in range(count)]

    def swap_off(x):
        return lax.ppermute(x, "mesh", off_route)

    def swap_on(x):
        return lax.ppermute(x, "mesh", on_route)

    def shape(*dims, dtype=BF16):
        return jax.ShapeDtypeStruct(dims, dtype)

    square = 2 * size * width * width
    pairs = (pair_target, pair_source, pair_count, obs_latent, pair_coupling)
    sums_off = swap_off(pair_sums("off", BF16, blocks, *pairs))
    sums_on = swap_on(pair_sums("on", BF16, blocks, *pairs))
    sums_own = pair_sums("self", F32, blocks, *pairs)
    pre, state_p, mix = call(
        prepare_kernel,
        (shape(size, width, dtype=F32), shape(size, width), shape(size, size + 2 * rows)),
        rim_send,
        neighbor,
        mesh_state,
        enc_gain[None],
        enc_self,
        mesh_coupling,
        specs=[SMEM, SMEM] + [VMEM] * 4,
        flops=2 * square,
        name="prepare",
    )
    state, normed = call(
        encode_kernel,
        (shape(size, width), shape(size, width)),
        rim_send,
        pre,
        state_p,
        sums_own,
        sums_on,
        sums_off,
        enc_obs,
        enc_out,
        node_gain[:1],
        specs=[SMEM] + [VMEM] * 8,
        flops=2 * square,
        name="encode",
    )
    rounds = node_gain.shape[0]
    for r in range(rounds):
        last = r == rounds - 1
        off = swap_off(normed[:rows])
        on = swap_on(normed[rows : 2 * rows])
        pre, message = call(
            local_kernel,
            (shape(size, width, dtype=F32), shape(size, width, dtype=F32)),
            normed,
            node_self[r],
            mix,
            flops=2 * square,
            name="local_part",
        )
        outs = call(
            lambda *refs, last=last: round_kernel(last, *refs),
            (shape(blocks, rows, width),) if last else (shape(size, width), shape(size, width)),
            rim_send,
            pre,
            message,
            mix,
            off,
            on,
            state,
            node_msg[r],
            node_out[r],
            node_gain[(r + 1) % rounds][None],
            specs=[SMEM] + [VMEM] * 9,
            flops=3 * square,
            name="round_rest",
        )
        if not last:
            state, normed = outs
    return outs[0]


def solution(mesh):
    block = P(("groups", "mesh"), None, None)
    return jax.shard_map(
        shards,
        mesh=mesh,
        in_specs=(
            block,
            block,
            block,
            P(("groups", "mesh")),
            P(("groups", "mesh")),
            P(("groups", "mesh")),
            P("mesh", None, None, None),
            P("mesh", None),
            P("mesh", None),
        )
        + (P(),) * 8,
        out_specs=block,
        check_vma=False,
    )
```

```python
import jax
import jax.numpy as jnp
from jax import lax
from jax.experimental import pallas as pl
from jax.experimental.pallas import tpu as pltpu
from jax.sharding import PartitionSpec as P

F32 = jnp.float32
BF16 = jnp.bfloat16
VMEM = pl.BlockSpec(memory_space=pltpu.VMEM)
SMEM = pl.BlockSpec(memory_space=pltpu.SMEM)
HBM = pl.BlockSpec(memory_space=pltpu.HBM)


def dot(a, b):
    return jnp.dot(a, b, preferred_element_type=F32)


def silu(v):
    half = 0.5 * v
    return half + half * jnp.tanh(half)


def norm_rows(values, gain):
    center = values - jnp.mean(values, axis=-1, keepdims=True)
    spread = jnp.mean(center * center, axis=-1, keepdims=True)
    return (center * lax.rsqrt(spread + 1e-05) * gain).astype(BF16)


def odd_device():
    return lax.rem(lax.axis_index("mesh"), 2)


def block_order(rim):
    odd = odd_device()
    off = rim[0, odd]
    on = rim[0, 1 - odd]
    low = jnp.minimum(off, on)
    high = jnp.maximum(off, on)
    third = jnp.where(low > 0, 0, jnp.where(high > 1, 1, 2))
    fourth = jnp.where(high < 3, 3, jnp.where(low < 2, 2, 1))
    return [off, on, third, fourth]


def pair_kernel(sides, cnt, tgt_hbm, src_hbm, obs, cpl, *refs):
    outs = refs[: len(sides)]
    tgt, src, isem, xbuf, cbuf, acc, xsem, csem = refs[-8:]
    blocks = outs[0].shape[0]
    odd = odd_device()
    parts = [{"off": 2 * odd, "on": 2 - 2 * odd, "self": 1}[side] for side in sides]
    reads = [
        pltpu.make_async_copy(a, b, isem.at[i])
        for i, (a, b) in enumerate(((tgt_hbm, tgt), (src_hbm, src)))
    ]
    for read in reads:
        read.start()
    for read in reads:
        read.wait()
    live = cnt[0]

    def group(e):
        t = tgt[e]
        mine, place = jnp.bool_(False), jnp.int32(0)
        for i, part in enumerate(parts):
            here = (t >= part * blocks) & (t < (part + 1) * blocks)
            mine = mine | here
            place = jnp.where(here, t - part * blocks + i * blocks, place)
        return place, mine

    groups = len(sides) * blocks

    def bump(words, place, mine):
        return [
            word + jnp.where(mine & (place // 4 == i), 1 << (8 * (place % 4)), 0)
            for i, word in enumerate(words)
        ]

    def count(e, words):
        return bump(words, *group(e))

    words = lax.fori_loop(0, live, count, [jnp.int32(0)] * (groups // 4))
    counts = [(words[g // 4] >> (8 * (g % 4))) & 255 for g in range(groups)]
    firsts, total = [], jnp.int32(0)
    for g in range(groups):
        firsts.append(total)
        total = total + counts[g]
    free = []
    for i in range(groups // 4):
        word = jnp.int32(0)
        for j in range(4):
            word = word + (firsts[4 * i + j] << (8 * j))
        free.append(word)

    def fetch(e, words):
        place, mine = group(e)
        word = words[0]
        for i in range(1, len(words)):
            word = jnp.where(place // 4 == i, words[i], word)

        @pl.when(mine)
        def _():
            slot = (word >> (8 * (place % 4))) & 255
            pltpu.make_async_copy(obs.at[src[e]], xbuf.at[slot], xsem.at[slot]).start()
            pltpu.make_async_copy(cpl.at[e], cbuf.at[slot], csem.at[slot]).start()

        return bump(words, place, mine)

    lax.fori_loop(0, live, fetch, free)

    def arrive(slot):
        pltpu.make_async_copy(obs.at[0], xbuf.at[slot], xsem.at[slot]).wait()
        pltpu.make_async_copy(cpl.at[0], cbuf.at[slot], csem.at[slot]).wait()

    for g in range(groups):
        acc[...] = jnp.zeros_like(acc)

        def two(j, carry):
            slot = firsts[g] + 2 * j
            arrive(slot)
            arrive(slot + 1)
            left = jnp.concatenate([cbuf[slot], cbuf[slot + 1]], axis=1)
            right = jnp.concatenate([xbuf[slot], xbuf[slot + 1]], axis=0)
            acc[...] += dot(left, right)
            return carry

        lax.fori_loop(0, counts[g] // 2, two, 0)

        @pl.when(counts[g] % 2 == 1)
        def _():
            slot = firsts[g] + counts[g] - 1
            arrive(slot)
            acc[...] += dot(cbuf[slot], xbuf[slot])

        out = outs[g // blocks]
        out[g % blocks] = acc[...].astype(out.dtype)


def pair_sums(sides, blocks, tgt, src, cnt, obs, cpl, after=None):
    slots, rows, width = tgt.shape[0], obs.shape[1], obs.shape[2]
    more = [] if after is None else [after]
    return pl.pallas_call(
        lambda *refs: pair_kernel(list(sides), *refs[:5], *refs[5 + len(more) :]),
        out_shape=[jax.ShapeDtypeStruct((blocks, rows, width), d) for d in sides.values()],
        in_specs=[SMEM] + [HBM] * 4 + [pl.BlockSpec(memory_space=pl.ANY)] * len(more),
        out_specs=[VMEM] * len(sides),
        scratch_shapes=[
            pltpu.SMEM((slots,), jnp.int32),
            pltpu.SMEM((slots,), jnp.int32),
            pltpu.SemaphoreType.DMA((2,)),
            pltpu.VMEM((slots, rows, width), BF16),
            pltpu.VMEM((slots, rows, rows), BF16),
            pltpu.VMEM((rows, width), F32),
            pltpu.SemaphoreType.DMA((slots,)),
            pltpu.SemaphoreType.DMA((slots,)),
        ],
        compiler_params=pltpu.CompilerParams(vmem_limit_bytes=12 << 20),
        cost_estimate=pl.CostEstimate(flops=1 << 20, bytes_accessed=1 << 30, transcendentals=0),
        name="pairs_" + "_".join(sides),
    )(cnt, *[pltpu.with_memory_space_constraint(x, pltpu.HBM) for x in (tgt, src, obs, cpl)], *more)


def call(kernel, out, scalars, arrays, name, weight=20):
    return pl.pallas_call(
        kernel,
        out_shape=out,
        in_specs=[SMEM] * len(scalars) + [VMEM] * len(arrays),
        out_specs=[VMEM] * len(out),
        compiler_params=pltpu.CompilerParams(vmem_limit_bytes=14 << 20),
        cost_estimate=pl.CostEstimate(flops=1 << weight, bytes_accessed=1 << 24, transcendentals=0),
        name=name,
    )(*scalars, *arrays)


def update(state, pre, incoming, w_in, w_out):
    hidden = silu(pre + dot(incoming, w_in)).astype(BF16)
    return (state.astype(F32) + dot(hidden, w_out)).astype(BF16)


def prepare_kernel(rim, nbr, state, gain, w_self, coupling, pre, state_p, mix):
    blocks, rows = state.shape[0], state.shape[1]
    order = block_order(rim)
    odd = odd_device()
    last = blocks + 1
    codes = [1 + o for o in order] + [last * odd, last - last * odd]
    for i, m in enumerate(order):
        cut = pl.ds(i * rows, rows)
        values = state[m]
        state_p[cut, :] = values
        pre[cut, :] = dot(norm_rows(values.astype(F32), gain[...]), w_self[...])
        for c, code in enumerate(codes):
            total = None
            for k in range(coupling.shape[1]):
                term = jnp.where(nbr[m, k] == code, coupling[m, k].astype(F32), 0.0)
                total = term if total is None else total + term
            mix[cut, c * rows : (c + 1) * rows] = total.astype(BF16)


def pack_kernel(rim, state_p, own, on, mix, packed):
    rows, width = own.shape[1], own.shape[2]
    size = state_p.shape[0]
    m = block_order(rim)[0]
    packed[:, :width] = state_p[:rows, :]
    packed[:, width : 2 * width] = (own[m] + on[m].astype(F32)).astype(BF16)
    packed[:, 2 * width : 2 * width + rows] = mix[:rows, size : size + rows]
    lane = lax.broadcasted_iota(jnp.int32, (rows, 128), 1)
    packed[:, 2 * width + rows :] = jnp.where(lane == m, 1.0, 0.0).astype(BF16)


def encode_kernel(half, rim, pre, state_p, own, on, off, w_obs, w_out, gain, state, normed, *rims):
    rows = own.shape[1]
    summed = jnp.concatenate(
        [
            (own[m] + on[m].astype(F32) + off[m].astype(F32)).astype(BF16)
            for m in block_order(rim)[2 * half : 2 * half + 2]
        ],
        axis=0,
    )
    cut = slice(2 * half * rows, 2 * (half + 1) * rows)
    updated = update(state_p[cut, :], pre[cut, :], summed, w_obs[...], w_out[...])
    state[...] = updated
    result = norm_rows(updated.astype(F32), gain[:1, :])
    normed[...] = result
    if rims:
        rims[0][...] = result[rows:, :]


def partial_kernel(mix, first, second, on, message):
    rows, size = on.shape[0], mix.shape[0]
    message[...] = (
        dot(mix[:rows, : 2 * rows], first[...])
        + dot(mix[:rows, 2 * rows : size], second[...])
        + dot(mix[:rows, size + rows :], on[...])
    ).astype(BF16)


def neighbour_kernel(packed, sent, first, gain, w_self, w_obs, w_out, node_gain, n_self, _, state, normed, pre, message):
    rows, width = state.shape
    own = packed[:, :width]
    summed = packed[:, width : 2 * width].astype(F32)
    for t in range(sent.shape[0]):
        mask = packed[:, 2 * width + rows + t : 2 * width + rows + t + 1].astype(F32)
        summed = summed + mask * sent[t].astype(F32)
    start = dot(norm_rows(own.astype(F32), gain[...]), w_self[...])
    updated = update(own, start, summed.astype(BF16), w_obs[...], w_out[...])
    state[...] = updated
    result = norm_rows(updated.astype(F32), node_gain[:1, :])
    normed[...] = result
    pre[...] = dot(result, n_self[0])
    message[...] = dot(packed[:, 2 * width : 2 * width + rows], first[:rows, :])


def round_kernel(mix, first, second, off, on, state_a, state_b, n_self, n_msg, n_out, gain, state, normed, rim):
    size = state.shape[0]
    rows = off.shape[0]
    heard = jnp.concatenate([first[...], second[...], off[...], on[...]], axis=0)
    for half, (base, own) in enumerate(((state_a, first), (state_b, second))):
        cut = slice(2 * half * rows, 2 * (half + 1) * rows)
        incoming = dot(mix[cut, :], heard).astype(BF16)
        updated = update(base[...], dot(own[...], n_self[0]), incoming, n_msg[0], n_out[0])
        state[cut, :] = updated
        result = norm_rows(updated.astype(F32), gain[1:2, :])
        normed[cut, :] = result
        if half == 0:
            rim[...] = result[rows:, :]


def local_kernel(mix, normed, n_self, pre, message):
    size = normed.shape[0]
    pre[...] = dot(normed[...], n_self[1])
    message[...] = dot(mix[:, :size], normed[...])


def last_kernel(
    rim, arrived, on, far_message, far_pre, far_state, mix, pre, message, state, n_msg, n_out, gain, out
):
    rows = arrived.shape[0]
    size = state.shape[0]
    incoming = (arrived[...].astype(F32) + far_message[...]).astype(BF16)
    far = update(far_state[...], far_pre[...], incoming, n_msg[0], n_out[0])
    far = norm_rows(far.astype(F32), gain[1:2, :])
    rims = jnp.concatenate([far, on[...]], axis=0)
    order = block_order(rim)
    for half in range(2):
        cut = slice(2 * half * rows, 2 * (half + 1) * rows)
        incoming = (message[cut, :] + dot(mix[cut, size:], rims)).astype(BF16)
        updated = update(state[cut, :], pre[cut, :], incoming, n_msg[1], n_out[1])
        out[order[2 * half]] = updated[:rows, :]
        out[order[2 * half + 1]] = updated[rows:, :]


def shards(
    mesh_state,
    obs_latent,
    pair_coupling,
    pair_target,
    pair_source,
    pair_count,
    mesh_coupling,
    neighbor,
    rim_send,
    enc_gain,
    enc_self,
    enc_obs,
    enc_out,
    node_gain,
    node_self,
    node_msg,
    node_out,
):
    blocks, rows, width = mesh_state.shape
    size = blocks * rows
    count = lax.axis_size("mesh")
    on_route = [(i, i ^ 1) for i in range(count)]
    off_route = [(i, (i + 1) % count if i % 2 else (i - 1) % count) for i in range(count)]

    def swap_off(x):
        return lax.ppermute(x, "mesh", off_route)

    def swap_on(x):
        return lax.ppermute(x, "mesh", on_route)

    def wide(n, dtype=BF16):
        return jax.ShapeDtypeStruct((n, width), dtype)

    enc_gain = enc_gain[None]
    pairs = (pair_target, pair_source, pair_count, obs_latent, pair_coupling)
    (sent,) = pair_sums({"off": BF16}, blocks, *pairs)
    sums_off = swap_off(sent)
    sent_on, sums_own = pair_sums({"on": BF16, "self": F32}, blocks, *pairs, after=sent)
    sums_on = swap_on(sent_on)
    pre, state_p, mix = call(
        prepare_kernel,
        [wide(size, F32), wide(size), jax.ShapeDtypeStruct((size, size + 2 * rows), BF16)],
        [rim_send, neighbor],
        [mesh_state, enc_gain, enc_self, mesh_coupling],
        "prepare",
        weight=40,
    )
    (packed,) = call(
        pack_kernel,
        [jax.ShapeDtypeStruct((rows, 2 * width + 2 * rows), BF16)],
        [rim_send],
        [state_p, sums_own, sums_on, mix],
        "pack",
    )
    packed = swap_off(packed)
    encode = (pre, state_p, sums_own, sums_on, sums_off, enc_obs, enc_out, node_gain)
    state_a, first, rim_on = call(
        lambda *refs: encode_kernel(0, *refs),
        [wide(2 * rows), wide(2 * rows), wide(rows)],
        [rim_send],
        encode,
        "encode_rims",
    )
    on = swap_on(rim_on)
    state_b, second = call(
        lambda *refs: encode_kernel(1, *refs),
        [wide(2 * rows), wide(2 * rows)],
        [rim_send],
        encode,
        "encode_others",
    )
    (message,) = call(partial_kernel, [wide(rows)], [], [mix, first, second, on], "rim_message")
    arrived = swap_off(message)
    far_state, far, far_pre, far_message = call(
        neighbour_kernel,
        [wide(rows), wide(rows), wide(rows, F32), wide(rows, F32)],
        [],
        [packed, sent, first, enc_gain, enc_self, enc_obs, enc_out, node_gain, node_self, message],
        "neighbour_rim",
    )
    state, normed, rim_on = call(
        round_kernel,
        [wide(size), wide(size), wide(rows)],
        [],
        [mix, first, second, far, on, state_a, state_b, node_self, node_msg, node_out, node_gain],
        "round_0",
    )
    on = swap_on(rim_on)
    pre, message = call(
        local_kernel,
        [wide(size, F32), wide(size, F32)],
        [],
        [mix, normed, node_self],
        "round_1_local",
    )
    (out,) = call(
        last_kernel,
        [jax.ShapeDtypeStruct((blocks, rows, width), BF16)],
        [rim_send],
        [arrived, on, far_message, far_pre, far_state, mix, pre, message, state, node_msg, node_out, node_gain],
        "round_1",
    )
    return out


def solution(mesh):
    block = P(("groups", "mesh"), None, None)
    return jax.shard_map(
        shards,
        mesh=mesh,
        in_specs=(
            block,
            block,
            block,
            P(("groups", "mesh")),
            P(("groups", "mesh")),
            P(("groups", "mesh")),
            P("mesh", None, None, None),
            P("mesh", None),
            P("mesh", None),
        )
        + (P(),) * 8,
        out_specs=block,
        check_vma=False,
    )
```

```python
import jax
import jax.numpy as jnp
from jax import lax
from jax.experimental import pallas as pl
from jax.experimental.pallas import tpu as pltpu
from jax.sharding import PartitionSpec as P

F32 = jnp.float32
BF16 = jnp.bfloat16
VMEM = pl.BlockSpec(memory_space=pltpu.VMEM)
SMEM = pl.BlockSpec(memory_space=pltpu.SMEM)
HBM = pl.BlockSpec(memory_space=pltpu.HBM)


def dot(a, b):
    return jnp.dot(a, b, preferred_element_type=F32)


def silu(v):
    half = 0.5 * v
    return half + half * jnp.tanh(half)


def norm_rows(values, gain):
    center = values - jnp.mean(values, axis=-1, keepdims=True)
    spread = jnp.mean(center * center, axis=-1, keepdims=True)
    return (center * lax.rsqrt(spread + 1e-05) * gain).astype(BF16)


def odd_device():
    return lax.rem(lax.axis_index("mesh"), 2)


def block_order(rim):
    odd = odd_device()
    off = rim[0, odd]
    on = rim[0, 1 - odd]
    low = jnp.minimum(off, on)
    high = jnp.maximum(off, on)
    third = jnp.where(low > 0, 0, jnp.where(high > 1, 1, 2))
    fourth = jnp.where(high < 3, 3, jnp.where(low < 2, 2, 1))
    return [off, on, third, fourth]


def pair_kernel(sides, cnt, tgt_hbm, src_hbm, obs, cpl, *refs):
    outs = refs[: len(sides)]
    tgt, src, listed, xbuf, cbuf, acc, isem, csem, xsem = refs[-9:]
    blocks, slots = outs[0].shape[0], xbuf.shape[0]
    odd = odd_device()
    parts = [{"off": 2 * odd, "on": 2 - 2 * odd, "self": 1}[side] for side in sides]
    reads = [
        pltpu.make_async_copy(tgt_hbm, tgt, isem.at[0]),
        pltpu.make_async_copy(src_hbm, src, isem.at[1]),
        pltpu.make_async_copy(cpl, cbuf, csem),
    ]
    for read in reads:
        read.start()
    reads[0].wait()
    reads[1].wait()
    groups = len(sides) * blocks

    def fetch(e, words):
        t = tgt[e]
        mine, group = jnp.bool_(False), jnp.int32(0)
        for i, part in enumerate(parts):
            here = (t >= part * blocks) & (t < (part + 1) * blocks)
            mine = mine | here
            group = jnp.where(here, t - part * blocks + i * blocks, group)
        word = words[0]
        for i in range(1, len(words)):
            word = jnp.where(group >= 4 * i, words[i], word)
        shift = 8 * (group & 3)

        @pl.when(mine)
        def _():
            pltpu.make_async_copy(obs.at[src[e]], xbuf.at[e], xsem.at[e]).start()
            listed[group * slots + ((word >> shift) & 255)] = e

        return [
            word + jnp.where(mine & (group >= 4 * i) & (group < 4 * i + 4), 1 << shift, 0)
            for i, word in enumerate(words)
        ]

    words = lax.fori_loop(0, cnt[0], fetch, [jnp.int32(0)] * (groups // 4))
    reads[2].wait()

    for g in range(groups):
        number = (words[g // 4] >> (8 * (g % 4))) & 255
        acc[...] = jnp.zeros_like(acc)

        def some(first, n):
            at = [listed[g * slots + first + i] for i in range(n)]
            for e in at:
                pltpu.make_async_copy(obs.at[0], xbuf.at[e], xsem.at[e]).wait()
            left = jnp.concatenate([cbuf[e] for e in at], axis=1)
            right = jnp.concatenate([xbuf[e] for e in at], axis=0)
            acc[...] += dot(left, right)

        def four(j, carry):
            some(4 * j, 4)
            return carry

        lax.fori_loop(0, number // 4, four, 0)
        for n in range(1, 4):

            @pl.when(number % 4 == n)
            def _():
                some(number - n, n)

        out = outs[g // blocks]
        out[g % blocks] = acc[...].astype(out.dtype)


def pair_sums(sides, blocks, tgt, src, cnt, obs, cpl, after=None):
    slots, rows, width = tgt.shape[0], obs.shape[1], obs.shape[2]
    more = [] if after is None else [after]
    return pl.pallas_call(
        lambda *refs: pair_kernel(list(sides), *refs[:5], *refs[5 + len(more) :]),
        out_shape=[jax.ShapeDtypeStruct((blocks, rows, width), d) for d in sides.values()],
        in_specs=[SMEM] + [HBM] * 4 + [pl.BlockSpec(memory_space=pl.ANY)] * len(more),
        out_specs=[VMEM] * len(sides),
        scratch_shapes=[
            pltpu.SMEM((slots,), jnp.int32),
            pltpu.SMEM((slots,), jnp.int32),
            pltpu.SMEM((len(sides) * blocks * slots,), jnp.int32),
            pltpu.VMEM((slots, rows, width), BF16),
            pltpu.VMEM((slots, rows, rows), BF16),
            pltpu.VMEM((rows, width), F32),
            pltpu.SemaphoreType.DMA((2,)),
            pltpu.SemaphoreType.DMA,
            pltpu.SemaphoreType.DMA((slots,)),
        ],
        compiler_params=pltpu.CompilerParams(vmem_limit_bytes=12 << 20),
        cost_estimate=pl.CostEstimate(flops=1 << 20, bytes_accessed=1 << 20, transcendentals=0),
        name="pairs_" + "_".join(sides),
    )(cnt, *[pltpu.with_memory_space_constraint(x, pltpu.HBM) for x in (tgt, src, obs, cpl)], *more)


def call(kernel, out, scalars, arrays, name, weight=20):
    return pl.pallas_call(
        kernel,
        out_shape=out,
        in_specs=[SMEM] * len(scalars) + [VMEM] * len(arrays),
        out_specs=[VMEM] * len(out),
        compiler_params=pltpu.CompilerParams(vmem_limit_bytes=14 << 20),
        cost_estimate=pl.CostEstimate(flops=1 << weight, bytes_accessed=1 << 20, transcendentals=0),
        name=name,
    )(*scalars, *arrays)


def update(state, pre, incoming, w_in, w_out):
    hidden = silu(pre + dot(incoming, w_in)).astype(BF16)
    return (state.astype(F32) + dot(hidden, w_out)).astype(BF16)


def prepare_kernel(rim, nbr, state, gain, w_self, coupling, pre, state_p, mix):
    blocks, rows = state.shape[0], state.shape[1]
    order = block_order(rim)
    odd = odd_device()
    last = blocks + 1
    codes = [1 + o for o in order] + [last * odd, last - last * odd]
    for i, m in enumerate(order):
        cut = pl.ds(i * rows, rows)
        values = state[m]
        state_p[cut, :] = values
        pre[cut, :] = dot(norm_rows(values.astype(F32), gain[...]), w_self[...])
        for c, code in enumerate(codes):
            total = None
            for k in range(coupling.shape[1]):
                term = jnp.where(nbr[m, k] == code, coupling[m, k].astype(F32), 0.0)
                total = term if total is None else total + term
            mix[cut, c * rows : (c + 1) * rows] = total.astype(BF16)


def encode_kernel(half, rim, pre, state_p, own, on, off, w_obs, w_out, gain, mix, state, normed, *rims):
    blocks, rows = own.shape[0], own.shape[1]
    summed = jnp.concatenate(
        [
            (own[m] + on[m].astype(F32) + off[m].astype(F32)).astype(BF16)
            for m in block_order(rim)[2 * half : 2 * half + 2]
        ],
        axis=0,
    )
    cut = slice(2 * half * rows, 2 * (half + 1) * rows)
    updated = update(state_p[cut, :], pre[cut, :], summed, w_obs[...], w_out[...])
    state[...] = updated
    result = norm_rows(updated.astype(F32), gain[:1, :])
    normed[...] = result
    if rims:
        width, size = state.shape[1], blocks * rows
        rims[0][...] = result[rows:, :]
        rims[1][:, :width] = updated[:rows, :]
        rims[1][:, width:] = mix[:rows, size : size + rows]


def partial_kernel(mix, first, second, on, message):
    rows, size = on.shape[0], mix.shape[0]
    message[...] = (
        dot(mix[:rows, : 2 * rows], first[...])
        + dot(mix[:rows, 2 * rows : size], second[...])
        + dot(mix[:rows, size + rows :], on[...])
    ).astype(BF16)


def neighbour_kernel(packed, first, node_gain, n_self, _, state, normed, pre, message):
    rows, width = state.shape
    values = packed[:, :width]
    state[...] = values
    result = norm_rows(values.astype(F32), node_gain[:1, :])
    normed[...] = result
    pre[...] = dot(result, n_self[0])
    message[...] = dot(packed[:, width:], first[:rows, :])


def round_kernel(mix, first, second, off, on, state_a, state_b, n_self, n_msg, n_out, gain, state, normed, rim):
    size = state.shape[0]
    rows = off.shape[0]
    heard = jnp.concatenate([first[...], second[...], off[...], on[...]], axis=0)
    for half, (base, own) in enumerate(((state_a, first), (state_b, second))):
        cut = slice(2 * half * rows, 2 * (half + 1) * rows)
        incoming = dot(mix[cut, :], heard).astype(BF16)
        updated = update(base[...], dot(own[...], n_self[0]), incoming, n_msg[0], n_out[0])
        state[cut, :] = updated
        result = norm_rows(updated.astype(F32), gain[1:2, :])
        normed[cut, :] = result
        if half == 0:
            rim[...] = result[rows:, :]


def local_kernel(mix, normed, n_self, pre, message):
    size = normed.shape[0]
    pre[...] = dot(normed[...], n_self[1])
    message[...] = dot(mix[:, :size], normed[...])


def last_kernel(
    rim, arrived, on, far_message, far_pre, far_state, mix, pre, message, state, n_msg, n_out, gain, out
):
    rows = arrived.shape[0]
    size = state.shape[0]
    incoming = (arrived[...].astype(F32) + far_message[...]).astype(BF16)
    far = update(far_state[...], far_pre[...], incoming, n_msg[0], n_out[0])
    far = norm_rows(far.astype(F32), gain[1:2, :])
    rims = jnp.concatenate([far, on[...]], axis=0)
    order = block_order(rim)
    for half in range(2):
        cut = slice(2 * half * rows, 2 * (half + 1) * rows)
        incoming = (message[cut, :] + dot(mix[cut, size:], rims)).astype(BF16)
        updated = update(state[cut, :], pre[cut, :], incoming, n_msg[1], n_out[1])
        out[order[2 * half]] = updated[:rows, :]
        out[order[2 * half + 1]] = updated[rows:, :]


def shards(
    mesh_state,
    obs_latent,
    pair_coupling,
    pair_target,
    pair_source,
    pair_count,
    mesh_coupling,
    neighbor,
    rim_send,
    enc_gain,
    enc_self,
    enc_obs,
    enc_out,
    node_gain,
    node_self,
    node_msg,
    node_out,
):
    blocks, rows, width = mesh_state.shape
    size = blocks * rows
    count = lax.axis_size("mesh")
    on_route = [(i, i ^ 1) for i in range(count)]
    off_route = [(i, (i + 1) % count if i % 2 else (i - 1) % count) for i in range(count)]

    def swap_off(x):
        return lax.ppermute(x, "mesh", off_route)

    def swap_on(x):
        return lax.ppermute(x, "mesh", on_route)

    def wide(n, dtype=BF16):
        return jax.ShapeDtypeStruct((n, width), dtype)

    enc_gain = enc_gain[None]
    pairs = (pair_target, pair_source, pair_count, obs_latent, pair_coupling)
    (sent,) = pair_sums({"off": BF16}, blocks, *pairs)
    sums_off = swap_off(sent)
    sent_on, sums_own = pair_sums({"on": BF16, "self": F32}, blocks, *pairs, after=sent)
    sums_on = swap_on(sent_on)
    pre, state_p, mix = call(
        prepare_kernel,
        [wide(size, F32), wide(size), jax.ShapeDtypeStruct((size, size + 2 * rows), BF16)],
        [rim_send, neighbor],
        [mesh_state, enc_gain, enc_self, mesh_coupling],
        "prepare",
        weight=34,
    )
    encode = (pre, state_p, sums_own, sums_on, sums_off, enc_obs, enc_out, node_gain, mix)
    state_a, first, rim_on, packed = call(
        lambda *refs: encode_kernel(0, *refs),
        [wide(2 * rows), wide(2 * rows), wide(rows), jax.ShapeDtypeStruct((rows, width + rows), BF16)],
        [rim_send],
        encode,
        "encode_rims",
    )
    on = swap_on(rim_on)
    packed = swap_off(packed)
    state_b, second = call(
        lambda *refs: encode_kernel(1, *refs),
        [wide(2 * rows), wide(2 * rows)],
        [rim_send],
        encode,
        "encode_others",
    )
    (message,) = call(partial_kernel, [wide(rows)], [], [mix, first, second, on], "rim_message")
    arrived = swap_off(message)
    far_state, far, far_pre, far_message = call(
        neighbour_kernel,
        [wide(rows), wide(rows), wide(rows, F32), wide(rows, F32)],
        [],
        [packed, first, node_gain, node_self, message],
        "neighbour_rim",
    )
    state, normed, rim_on = call(
        round_kernel,
        [wide(size), wide(size), wide(rows)],
        [],
        [mix, first, second, far, on, state_a, state_b, node_self, node_msg, node_out, node_gain],
        "round_0",
    )
    on = swap_on(rim_on)
    pre, message = call(
        local_kernel,
        [wide(size, F32), wide(size, F32)],
        [],
        [mix, normed, node_self],
        "round_1_local",
    )
    (out,) = call(
        last_kernel,
        [jax.ShapeDtypeStruct((blocks, rows, width), BF16)],
        [rim_send],
        [arrived, on, far_message, far_pre, far_state, mix, pre, message, state, node_msg, node_out, node_gain],
        "round_1",
    )
    return out


def solution(mesh):
    block = P(("groups", "mesh"), None, None)
    return jax.shard_map(
        shards,
        mesh=mesh,
        in_specs=(
            block,
            block,
            block,
            P(("groups", "mesh")),
            P(("groups", "mesh")),
            P(("groups", "mesh")),
            P("mesh", None, None, None),
            P("mesh", None),
            P("mesh", None),
        )
        + (P(),) * 8,
        out_specs=block,
        check_vma=False,
    )
```

```python
import jax
import jax.numpy as jnp
from jax import lax
from jax.experimental import pallas as pl
from jax.experimental.pallas import tpu as pltpu
from jax.sharding import PartitionSpec as P

F32 = jnp.float32
BF16 = jnp.bfloat16
VMEM = pl.BlockSpec(memory_space=pltpu.VMEM)
SMEM = pl.BlockSpec(memory_space=pltpu.SMEM)
HBM = pl.BlockSpec(memory_space=pltpu.HBM)


def dot(a, b):
    return jnp.dot(a, b, preferred_element_type=F32)


def silu(v):
    half = 0.5 * v
    return half + half * jnp.tanh(half)


def norm_rows(values, gain):
    center = values - jnp.mean(values, axis=-1, keepdims=True)
    spread = jnp.mean(center * center, axis=-1, keepdims=True)
    return (center * lax.rsqrt(spread + 1e-05) * gain).astype(BF16)


def odd_device():
    return lax.rem(lax.axis_index("mesh"), 2)


def pair_kernel(sides, cnt, tgt_hbm, src_hbm, obs, cpl, *refs):
    outs = refs[: len(sides)]
    tgt, src, listed, xbuf, cbuf, acc, isem, csem, xsem = refs[-9:]
    blocks, slots = outs[0].shape[0], xbuf.shape[0]
    odd = odd_device()
    parts = [{"off": 2 * odd, "on": 2 - 2 * odd, "self": 1}[side] for side in sides]
    reads = [
        pltpu.make_async_copy(tgt_hbm, tgt, isem.at[0]),
        pltpu.make_async_copy(src_hbm, src, isem.at[1]),
        pltpu.make_async_copy(cpl, cbuf, csem),
    ]
    for read in reads:
        read.start()
    reads[0].wait()
    reads[1].wait()
    groups = len(sides) * blocks

    def fetch(e, words):
        t = tgt[e]
        mine, group = jnp.bool_(False), jnp.int32(0)
        for i, part in enumerate(parts):
            here = (t >= part * blocks) & (t < (part + 1) * blocks)
            mine = mine | here
            group = jnp.where(here, t - part * blocks + i * blocks, group)
        word = words[0]
        for i in range(1, len(words)):
            word = jnp.where(group >= 4 * i, words[i], word)
        shift = 8 * (group & 3)

        @pl.when(mine)
        def _():
            pltpu.make_async_copy(obs.at[src[e]], xbuf.at[e], xsem.at[e]).start()
            listed[group * slots + ((word >> shift) & 255)] = e

        return [
            word + jnp.where(mine & (group >= 4 * i) & (group < 4 * i + 4), 1 << shift, 0)
            for i, word in enumerate(words)
        ]

    words = lax.fori_loop(0, cnt[0], fetch, [jnp.int32(0)] * (groups // 4))
    reads[2].wait()

    for g in range(groups):
        number = (words[g // 4] >> (8 * (g % 4))) & 255
        def some(first, n):
            at = [listed[g * slots + first + i] for i in range(n)]
            for e in at:
                pltpu.make_async_copy(obs.at[0], xbuf.at[e], xsem.at[e]).wait()
            left = jnp.concatenate([cbuf[e] for e in at], axis=1)
            right = jnp.concatenate([xbuf[e] for e in at], axis=0)
            return dot(left, right)

        @pl.when(number % 4 == 0)
        def _():
            acc[...] = jnp.zeros_like(acc)

        for n in range(1, 4):

            @pl.when(number % 4 == n)
            def _():
                acc[...] = some(0, n)

        def four(j, carry):
            acc[...] += some(number % 4 + 4 * j, 4)
            return carry

        lax.fori_loop(0, number // 4, four, 0)

        out = outs[g // blocks]
        out[g % blocks] = acc[...].astype(out.dtype)


def pair_sums(sides, blocks, tgt, src, cnt, obs, cpl, after=None):
    slots, rows, width = tgt.shape[0], obs.shape[1], obs.shape[2]
    more = [] if after is None else [after]
    return pl.pallas_call(
        lambda *refs: pair_kernel(list(sides), *refs[:5], *refs[5 + len(more) :]),
        out_shape=[jax.ShapeDtypeStruct((blocks, rows, width), d) for d in sides.values()],
        in_specs=[SMEM] + [HBM] * 4 + [pl.BlockSpec(memory_space=pl.ANY)] * len(more),
        out_specs=[VMEM] * len(sides),
        scratch_shapes=[
            pltpu.SMEM((slots,), jnp.int32),
            pltpu.SMEM((slots,), jnp.int32),
            pltpu.SMEM((len(sides) * blocks * slots,), jnp.int32),
            pltpu.VMEM((slots, rows, width), BF16),
            pltpu.VMEM((slots, rows, rows), BF16),
            pltpu.VMEM((rows, width), F32),
            pltpu.SemaphoreType.DMA((2,)),
            pltpu.SemaphoreType.DMA,
            pltpu.SemaphoreType.DMA((slots,)),
        ],
        compiler_params=pltpu.CompilerParams(vmem_limit_bytes=12 << 20),
        cost_estimate=pl.CostEstimate(flops=1 << 20, bytes_accessed=1 << 20, transcendentals=0),
        name="pairs_" + "_".join(sides),
    )(cnt, *[pltpu.with_memory_space_constraint(x, pltpu.HBM) for x in (tgt, src, obs, cpl)], *more)


def call(kernel, out, arrays, name, scalars=(), late=(), weight=20, place=VMEM, scratch=()):
    return pl.pallas_call(
        kernel,
        out_shape=out,
        in_specs=[SMEM] * len(scalars) + [pl.BlockSpec(memory_space=pl.ANY)] * len(late) + [VMEM] * len(arrays),
        out_specs=[place] * len(out),
        scratch_shapes=list(scratch),
        compiler_params=pltpu.CompilerParams(vmem_limit_bytes=14 << 20),
        cost_estimate=pl.CostEstimate(flops=1 << weight, bytes_accessed=1 << 20, transcendentals=0),
        name=name,
    )(*scalars, *late, *arrays)


def read_rim(rim_ref, rim, sem):
    copy = pltpu.make_async_copy(rim_ref, rim, sem)
    copy.start()

    def get():
        copy.wait()
        odd = odd_device()
        return rim[0, odd], rim[0, 1 - odd]

    return get


RIM = (pltpu.SMEM((1, 2), jnp.int32), pltpu.SemaphoreType.DMA)


def updates(states, pres, incoming, w_in, w_out):
    first = [dot(x, w_in) for x in incoming]
    hidden = [silu(p + x).astype(BF16) for p, x in zip(pres, first)]
    second = [dot(x, w_out) for x in hidden]
    return [(s.astype(F32) + x).astype(BF16) for s, x in zip(states, second)]


def prepare_kernel(nbr, state, gain, w_self, coupling, pre, mix):
    blocks, rows = state.shape[0], state.shape[1]
    odd = odd_device()
    last = blocks + 1
    codes = [1 + c for c in range(blocks)] + [last * odd, last - last * odd]
    for m in range(blocks):
        pre[m] = dot(norm_rows(state[m].astype(F32), gain[...]), w_self[...])
        for c, code in enumerate(codes):
            total = None
            for k in range(coupling.shape[1]):
                term = jnp.where(nbr[m, k] == code, coupling[m, k].astype(F32), 0.0)
                total = term if total is None else total + term
            mix[m, :, c * rows : (c + 1) * rows] = total.astype(BF16)


def encode_kernel(
    rim_ref, pre, base, own, on, off, w_obs, w_out, gain, mix, state, normed, rim_on, rim_off, packed, row, rim, sem
):
    blocks, rows, width = own.shape
    rims = read_rim(rim_ref, rim, sem)
    summed = [(own[m] + on[m].astype(F32) + off[m].astype(F32)).astype(BF16) for m in range(blocks)]
    each = range(blocks)
    updated = updates([base[m] for m in each], [pre[m] for m in each], summed, w_obs[...], w_out[...])
    for m in each:
        state[m] = updated[m]
        normed[m] = norm_rows(updated[m].astype(F32), gain[:1, :])
    off_rim, on_rim = rims()
    rim_on[...] = normed[on_rim]
    rim_off[...] = normed[off_rim]
    size = blocks * rows
    packed[:, :width] = state[off_rim]
    packed[:, width:] = mix[off_rim, :, size : size + rows]
    row[...] = mix[off_rim]


def part_kernel(row, normed, part):
    blocks, rows, width = normed.shape
    size = blocks * rows
    part[...] = dot(row[:, :size], normed[...].reshape(size, width))


def message_kernel(row, part, on, message):
    message[...] = (part[...] + dot(row[:, row.shape[1] - on.shape[0] :], on[...])).astype(BF16)


def neighbour_kernel(packed, rim_off, node_gain, n_self, _, state, normed, pre, message):
    rows, width = state.shape
    values = packed[:, :width]
    state[...] = values
    result = norm_rows(values.astype(F32), node_gain[:1, :])
    normed[...] = result
    pre[...] = dot(result, n_self[0])
    message[...] = dot(packed[:, width:], rim_off[...])


def round_kernel(rim_ref, mix, normed, off, on, state, n_self, n_msg, n_out, gain, new_state, new_normed, rim_on, rim, sem):
    blocks, rows, width = state.shape
    rims = read_rim(rim_ref, rim, sem)
    size = blocks * rows
    own = normed[...].reshape(size, width)
    heard = jnp.concatenate([own, off[...], on[...]], axis=0)
    each = range(blocks)
    pre = [dot(normed[m], n_self[0]) for m in each]
    incoming = [dot(mix[m], heard).astype(BF16) for m in each]
    updated = updates([state[m] for m in each], pre, incoming, n_msg[0], n_out[0])
    for m in each:
        new_state[m] = updated[m]
        new_normed[m] = norm_rows(updated[m].astype(F32), gain[1:2, :])
    rim_on[...] = new_normed[rims()[1]]


def local_kernel(mix, normed, n_self, pre, message):
    blocks, rows, width = normed.shape
    size = blocks * rows
    own = normed[...].reshape(size, width)
    pre[...] = dot(own, n_self[1]).reshape(pre.shape)
    message[...] = dot(mix[...].reshape(size, -1)[:, :size], own).reshape(message.shape)


def last_kernel(
    arrived, on, far_message, far_pre, far_state, mix, pre, message, state, n_msg, n_out, gain, out, stage, sems
):
    blocks, rows, width = state.shape
    size = blocks * rows
    incoming = (arrived[...].astype(F32) + far_message[...]).astype(BF16)
    (far,) = updates([far_state[...]], [far_pre[...]], [incoming], n_msg[0], n_out[0])
    far = norm_rows(far.astype(F32), gain[1:2, :])
    rims = jnp.concatenate([far, on[...]], axis=0)
    each = range(blocks)
    incoming = [(message[m] + dot(mix[m, :, size:], rims)).astype(BF16) for m in each]
    updated = updates([state[m] for m in each], [pre[m] for m in each], incoming, n_msg[1], n_out[1])
    copies = [pltpu.make_async_copy(stage.at[m], out.at[m], sems.at[m]) for m in each]
    for m in each:
        stage[m] = updated[m]
        copies[m].start()
    for copy in copies:
        copy.wait()


def shards(
    mesh_state,
    obs_latent,
    pair_coupling,
    pair_target,
    pair_source,
    pair_count,
    mesh_coupling,
    neighbor,
    rim_send,
    enc_gain,
    enc_self,
    enc_obs,
    enc_out,
    node_gain,
    node_self,
    node_msg,
    node_out,
):
    blocks, rows, width = mesh_state.shape
    size = blocks * rows
    count = lax.axis_size("mesh")
    on_route = [(i, i ^ 1) for i in range(count)]
    off_route = [(i, (i + 1) % count if i % 2 else (i - 1) % count) for i in range(count)]

    def swap_off(x):
        return lax.ppermute(x, "mesh", off_route)

    def swap_on(x):
        return lax.ppermute(x, "mesh", on_route)

    def shape(*dims, dtype=BF16):
        return jax.ShapeDtypeStruct(dims, dtype)

    whole, block = (blocks, rows, width), (rows, width)
    pairs = (pair_target, pair_source, pair_count, obs_latent, pair_coupling)
    (sent,) = pair_sums({"off": BF16}, blocks, *pairs)
    sums_off = swap_off(sent)
    sent_on, sums_own = pair_sums({"on": BF16, "self": F32}, blocks, *pairs, after=sent)
    sums_on = swap_on(sent_on)
    pre, mix = call(
        prepare_kernel,
        [shape(*whole, dtype=F32), shape(blocks, rows, size + 2 * rows)],
        [mesh_state, enc_gain[None], enc_self, mesh_coupling],
        "prepare",
        scalars=[neighbor],
        weight=34,
    )
    state, normed, rim_on, rim_off, packed, row = call(
        encode_kernel,
        [
            shape(*whole),
            shape(*whole),
            shape(*block),
            shape(*block),
            shape(rows, width + rows),
            shape(rows, size + 2 * rows),
        ],
        [pre, mesh_state, sums_own, sums_on, sums_off, enc_obs, enc_out, node_gain, mix],
        "encode",
        late=[rim_send],
        scratch=RIM,
    )
    packed = swap_off(packed)
    on = swap_on(rim_on)
    (part,) = call(part_kernel, [shape(*block, dtype=F32)], [row, normed], "rim_part")
    (message,) = call(message_kernel, [shape(*block)], [row, part, on], "rim_message")
    arrived = swap_off(message)
    far_state, far, far_pre, far_message = call(
        neighbour_kernel,
        [shape(*block), shape(*block), shape(*block, dtype=F32), shape(*block, dtype=F32)],
        [packed, rim_off, node_gain, node_self, message],
        "neighbour_rim",
    )
    state, normed, rim_on = call(
        round_kernel,
        [shape(*whole), shape(*whole), shape(*block)],
        [mix, normed, far, on, state, node_self, node_msg, node_out, node_gain],
        "round_0",
        late=[rim_send],
        scratch=RIM,
    )
    on = swap_on(rim_on)
    pre, message = call(
        local_kernel,
        [shape(*whole, dtype=F32), shape(*whole, dtype=F32)],
        [mix, normed, node_self],
        "round_1_local",
    )
    (out,) = call(
        last_kernel,
        [shape(*whole)],
        [arrived, on, far_message, far_pre, far_state, mix, pre, message, state, node_msg, node_out, node_gain],
        "round_1",
        place=HBM,
        scratch=[pltpu.VMEM(whole, BF16), pltpu.SemaphoreType.DMA((blocks,))],
    )
    return out


def solution(mesh):
    block = P(("groups", "mesh"), None, None)
    return jax.shard_map(
        shards,
        mesh=mesh,
        in_specs=(
            block,
            block,
            block,
            P(("groups", "mesh")),
            P(("groups", "mesh")),
            P(("groups", "mesh")),
            P("mesh", None, None, None),
            P("mesh", None),
            P("mesh", None),
        )
        + (P(),) * 8,
        out_specs=block,
        check_vma=False,
    )
```

```python
import jax
import jax.numpy as jnp
from jax import lax
from jax.experimental import pallas as pl
from jax.experimental.pallas import tpu as pltpu
from jax.sharding import PartitionSpec as P

F32 = jnp.float32
BF16 = jnp.bfloat16
VMEM = pl.BlockSpec(memory_space=pltpu.VMEM)
SMEM = pl.BlockSpec(memory_space=pltpu.SMEM)
HBM = pl.BlockSpec(memory_space=pltpu.HBM)


def dot(a, b):
    return jnp.dot(a, b, preferred_element_type=F32)


def silu(v):
    half = 0.5 * v
    return half + half * jnp.tanh(half)


def norm_rows(values, gain):
    center = values - jnp.mean(values, axis=-1, keepdims=True)
    spread = jnp.mean(center * center, axis=-1, keepdims=True)
    return (center * lax.rsqrt(spread + 1e-05) * gain).astype(BF16)


def odd_device():
    return lax.rem(lax.axis_index("mesh"), 2)


def pair_kernel(sides, cnt, tgt_hbm, src_hbm, obs, cpl, *refs):
    outs = refs[: len(sides)]
    tgt, src, listed, xbuf, cbuf, acc, isem, csem, xsem = refs[-9:]
    blocks, slots = outs[0].shape[0], xbuf.shape[0]
    odd = odd_device()
    parts = [{"off": 2 * odd, "on": 2 - 2 * odd, "self": 1}[side] for side in sides]
    reads = [
        pltpu.make_async_copy(tgt_hbm, tgt, isem.at[0]),
        pltpu.make_async_copy(src_hbm, src, isem.at[1]),
        pltpu.make_async_copy(cpl, cbuf, csem),
    ]
    for read in reads:
        read.start()
    reads[0].wait()
    reads[1].wait()
    groups = len(sides) * blocks

    def fetch(e, words):
        t = tgt[e]
        mine, group = jnp.bool_(False), jnp.int32(0)
        for i, part in enumerate(parts):
            here = (t >= part * blocks) & (t < (part + 1) * blocks)
            mine = mine | here
            group = jnp.where(here, t - part * blocks + i * blocks, group)
        word = words[0]
        for i in range(1, len(words)):
            word = jnp.where(group >= 4 * i, words[i], word)
        shift = 8 * (group & 3)

        @pl.when(mine)
        def _():
            pltpu.make_async_copy(obs.at[src[e]], xbuf.at[e], xsem.at[e]).start()
            listed[group * slots + ((word >> shift) & 255)] = e

        return [
            word + jnp.where(mine & (group >= 4 * i) & (group < 4 * i + 4), 1 << shift, 0)
            for i, word in enumerate(words)
        ]

    words = lax.fori_loop(0, cnt[0], fetch, [jnp.int32(0)] * (groups // 4))
    reads[2].wait()

    for g in range(groups):
        number = (words[g // 4] >> (8 * (g % 4))) & 255
        def some(first, n):
            at = [listed[g * slots + first + i] for i in range(n)]
            for e in at:
                pltpu.make_async_copy(obs.at[0], xbuf.at[e], xsem.at[e]).wait()
            left = jnp.concatenate([cbuf[e] for e in at], axis=1)
            right = jnp.concatenate([xbuf[e] for e in at], axis=0)
            return dot(left, right)

        @pl.when(number % 4 == 0)
        def _():
            acc[...] = jnp.zeros_like(acc)

        for n in range(1, 4):

            @pl.when(number % 4 == n)
            def _():
                acc[...] = some(0, n)

        def four(j, carry):
            acc[...] += some(number % 4 + 4 * j, 4)
            return carry

        lax.fori_loop(0, number // 4, four, 0)

        out = outs[g // blocks]
        out[g % blocks] = acc[...].astype(out.dtype)


def pair_sums(sides, blocks, tgt, src, cnt, obs, cpl, after=None):
    slots, rows, width = tgt.shape[0], obs.shape[1], obs.shape[2]
    more = [] if after is None else [after]
    return pl.pallas_call(
        lambda *refs: pair_kernel(list(sides), *refs[:5], *refs[5 + len(more) :]),
        out_shape=[jax.ShapeDtypeStruct((blocks, rows, width), d) for d in sides.values()],
        in_specs=[SMEM] + [HBM] * 4 + [pl.BlockSpec(memory_space=pl.ANY)] * len(more),
        out_specs=[VMEM] * len(sides),
        scratch_shapes=[
            pltpu.SMEM((slots,), jnp.int32),
            pltpu.SMEM((slots,), jnp.int32),
            pltpu.SMEM((len(sides) * blocks * slots,), jnp.int32),
            pltpu.VMEM((slots, rows, width), BF16),
            pltpu.VMEM((slots, rows, rows), BF16),
            pltpu.VMEM((rows, width), F32),
            pltpu.SemaphoreType.DMA((2,)),
            pltpu.SemaphoreType.DMA,
            pltpu.SemaphoreType.DMA((slots,)),
        ],
        compiler_params=pltpu.CompilerParams(vmem_limit_bytes=12 << 20),
        cost_estimate=pl.CostEstimate(flops=1 << 20, bytes_accessed=1 << 20, transcendentals=0),
        name="pairs_" + "_".join(sides),
    )(cnt, *[pltpu.with_memory_space_constraint(x, pltpu.HBM) for x in (tgt, src, obs, cpl)], *more)


def call(kernel, out, arrays, name, scalars=(), late=(), weight=20, place=VMEM, scratch=()):
    return pl.pallas_call(
        kernel,
        out_shape=out,
        in_specs=[SMEM] * len(scalars) + [pl.BlockSpec(memory_space=pl.ANY)] * len(late) + [VMEM] * len(arrays),
        out_specs=[place] * len(out),
        scratch_shapes=list(scratch),
        compiler_params=pltpu.CompilerParams(vmem_limit_bytes=14 << 20),
        cost_estimate=pl.CostEstimate(flops=1 << weight, bytes_accessed=1 << 20, transcendentals=0),
        name=name,
    )(*scalars, *late, *arrays)


def read_rim(rim_ref, rim, sem):
    copy = pltpu.make_async_copy(rim_ref, rim, sem)
    copy.start()

    def get():
        copy.wait()
        odd = odd_device()
        return rim[0, odd], rim[0, 1 - odd]

    return get


RIM = (pltpu.SMEM((1, 2), jnp.int32), pltpu.SemaphoreType.DMA)


def updates(states, pres, incoming, w_in, w_out):
    first = [dot(x, w_in) for x in incoming]
    hidden = [silu(p + x).astype(BF16) for p, x in zip(pres, first)]
    second = [dot(x, w_out) for x in hidden]
    return [(s.astype(F32) + x).astype(BF16) for s, x in zip(states, second)]


def prepare_kernel(nbr, state, gain, w_self, coupling, pre, mix):
    blocks, rows = state.shape[0], state.shape[1]
    odd = odd_device()
    last = blocks + 1
    codes = [1 + c for c in range(blocks)] + [last * odd, last - last * odd]
    for m in range(blocks):
        pre[m] = dot(norm_rows(state[m].astype(F32), gain[...]), w_self[...])
        for c, code in enumerate(codes):
            total = None
            for k in range(coupling.shape[1]):
                term = jnp.where(nbr[m, k] == code, coupling[m, k].astype(F32), 0.0)
                total = term if total is None else total + term
            mix[m, :, c * rows : (c + 1) * rows] = total.astype(BF16)


def encode_kernel(
    rim_ref, pre, base, own, on, off, w_obs, w_out, gain, mix, state, normed, rim_on, rim_off, packed, row, rim, sem
):
    blocks, rows, width = own.shape
    rims = read_rim(rim_ref, rim, sem)
    summed = [(own[m] + on[m].astype(F32) + off[m].astype(F32)).astype(BF16) for m in range(blocks)]
    each = range(blocks)
    updated = updates([base[m] for m in each], [pre[m] for m in each], summed, w_obs[...], w_out[...])
    for m in each:
        state[m] = updated[m]
        normed[m] = norm_rows(updated[m].astype(F32), gain[:1, :])
    off_rim, on_rim = rims()
    rim_on[...] = normed[on_rim]
    rim_off[...] = normed[off_rim]
    size = blocks * rows
    packed[:, :width] = state[off_rim]
    packed[:, width:] = mix[off_rim, :, size : size + rows]
    row[...] = mix[off_rim]


def part_kernel(row, normed, part):
    blocks, rows, width = normed.shape
    size = blocks * rows
    part[...] = dot(row[:, :size], normed[...].reshape(size, width))


def message_kernel(row, part, on, _, message):
    message[...] = (part[...] + dot(row[:, row.shape[1] - on.shape[0] :], on[...])).astype(BF16)


def neighbour_kernel(packed, rim_off, node_gain, n_self, _, state, normed, pre, message):
    rows, width = state.shape
    values = packed[:, :width]
    state[...] = values
    result = norm_rows(values.astype(F32), node_gain[:1, :])
    normed[...] = result
    pre[...] = dot(result, n_self[0])
    message[...] = dot(packed[:, width:], rim_off[...])


def round_kernel(rim_ref, mix, off, on, pre, heard, state, n_msg, n_out, gain, new_state, new_normed, rim_on, rim, sem):
    blocks, rows, width = state.shape
    rims = read_rim(rim_ref, rim, sem)
    size = blocks * rows
    sides = jnp.concatenate([off[...], on[...]], axis=0)
    each = range(blocks)
    incoming = [(heard[m] + dot(mix[m, :, size:], sides)).astype(BF16) for m in each]
    updated = updates([state[m] for m in each], [pre[m] for m in each], incoming, n_msg[0], n_out[0])
    for m in each:
        new_state[m] = updated[m]
        new_normed[m] = norm_rows(updated[m].astype(F32), gain[1:2, :])
    rim_on[...] = new_normed[rims()[1]]


def local_kernel(r, mix, normed, n_self, pre, message):
    blocks, rows, width = normed.shape
    size = blocks * rows
    own = normed[...].reshape(size, width)
    pre[...] = dot(own, n_self[r]).reshape(pre.shape)
    message[...] = dot(mix[...].reshape(size, -1)[:, :size], own).reshape(message.shape)


def far_kernel(arrived, far_message, pre, state, n_msg, n_out, gain, normed):
    incoming = (arrived[...].astype(F32) + far_message[...]).astype(BF16)
    (updated,) = updates([state[...]], [pre[...]], [incoming], n_msg[0], n_out[0])
    normed[...] = norm_rows(updated.astype(F32), gain[1:2, :])


def last_kernel(far, on, mix, pre, message, state, n_msg, n_out, out, stage, sems):
    blocks, rows, width = state.shape
    size = blocks * rows
    rims = jnp.concatenate([far[...], on[...]], axis=0)
    each = range(blocks)
    incoming = [(message[m] + dot(mix[m, :, size:], rims)).astype(BF16) for m in each]
    updated = updates([state[m] for m in each], [pre[m] for m in each], incoming, n_msg[1], n_out[1])
    copies = [pltpu.make_async_copy(stage.at[m], out.at[m], sems.at[m]) for m in each]
    for m in each:
        stage[m] = updated[m]
        copies[m].start()
    for copy in copies:
        copy.wait()


def shards(
    mesh_state,
    obs_latent,
    pair_coupling,
    pair_target,
    pair_source,
    pair_count,
    mesh_coupling,
    neighbor,
    rim_send,
    enc_gain,
    enc_self,
    enc_obs,
    enc_out,
    node_gain,
    node_self,
    node_msg,
    node_out,
):
    blocks, rows, width = mesh_state.shape
    size = blocks * rows
    count = lax.axis_size("mesh")
    on_route = [(i, i ^ 1) for i in range(count)]
    off_route = [(i, (i + 1) % count if i % 2 else (i - 1) % count) for i in range(count)]

    def swap_off(x):
        return lax.ppermute(x, "mesh", off_route)

    def swap_on(x):
        return lax.ppermute(x, "mesh", on_route)

    def shape(*dims, dtype=BF16):
        return jax.ShapeDtypeStruct(dims, dtype)

    whole, block = (blocks, rows, width), (rows, width)
    pairs = (pair_target, pair_source, pair_count, obs_latent, pair_coupling)
    (sent,) = pair_sums({"off": BF16}, blocks, *pairs)
    sums_off = swap_off(sent)
    sent_on, sums_own = pair_sums({"on": BF16, "self": F32}, blocks, *pairs, after=sent)
    sums_on = swap_on(sent_on)
    pre, mix = call(
        prepare_kernel,
        [shape(*whole, dtype=F32), shape(blocks, rows, size + 2 * rows)],
        [mesh_state, enc_gain[None], enc_self, mesh_coupling],
        "prepare",
        scalars=[neighbor],
        weight=34,
    )
    state, normed, rim_on, rim_off, packed, row = call(
        encode_kernel,
        [
            shape(*whole),
            shape(*whole),
            shape(*block),
            shape(*block),
            shape(rows, width + rows),
            shape(rows, size + 2 * rows),
        ],
        [pre, mesh_state, sums_own, sums_on, sums_off, enc_obs, enc_out, node_gain, mix],
        "encode",
        late=[rim_send],
        scratch=RIM,
    )
    packed = swap_off(packed)
    on = swap_on(rim_on)
    (part,) = call(part_kernel, [shape(*block, dtype=F32)], [row, normed], "rim_part")
    pre, heard = call(
        lambda *refs: local_kernel(0, *refs),
        [shape(*whole, dtype=F32), shape(*whole, dtype=F32)],
        [mix, normed, node_self],
        "round_0_local",
    )
    (message,) = call(message_kernel, [shape(*block)], [row, part, on, heard], "rim_message")
    arrived = swap_off(message)
    far_state, far, far_pre, far_message = call(
        neighbour_kernel,
        [shape(*block), shape(*block), shape(*block, dtype=F32), shape(*block, dtype=F32)],
        [packed, rim_off, node_gain, node_self, message],
        "neighbour_rim",
    )
    state, normed, rim_on = call(
        round_kernel,
        [shape(*whole), shape(*whole), shape(*block)],
        [mix, far, on, pre, heard, state, node_msg, node_out, node_gain],
        "round_0",
        late=[rim_send],
        scratch=RIM,
    )
    on = swap_on(rim_on)
    pre, message = call(
        lambda *refs: local_kernel(1, *refs),
        [shape(*whole, dtype=F32), shape(*whole, dtype=F32)],
        [mix, normed, node_self],
        "round_1_local",
    )
    (far,) = call(
        far_kernel,
        [shape(*block)],
        [arrived, far_message, far_pre, far_state, node_msg, node_out, node_gain],
        "far_rim",
    )
    (out,) = call(
        last_kernel,
        [shape(*whole)],
        [far, on, mix, pre, message, state, node_msg, node_out],
        "round_1",
        place=HBM,
        scratch=[pltpu.VMEM(whole, BF16), pltpu.SemaphoreType.DMA((blocks,))],
    )
    return out


def solution(mesh):
    block = P(("groups", "mesh"), None, None)
    return jax.shard_map(
        shards,
        mesh=mesh,
        in_specs=(
            block,
            block,
            block,
            P(("groups", "mesh")),
            P(("groups", "mesh")),
            P(("groups", "mesh")),
            P("mesh", None, None, None),
            P("mesh", None),
            P("mesh", None),
        )
        + (P(),) * 8,
        out_specs=block,
        check_vma=False,
    )
```

```python
import jax
import jax.numpy as jnp
from jax import lax
from jax.experimental import pallas as pl
from jax.experimental.pallas import tpu as pltpu
from jax.sharding import PartitionSpec as P

F32 = jnp.float32
BF16 = jnp.bfloat16
VMEM = pl.BlockSpec(memory_space=pltpu.VMEM)
SMEM = pl.BlockSpec(memory_space=pltpu.SMEM)
HBM = pl.BlockSpec(memory_space=pltpu.HBM)


def dot(a, b):
    return jnp.dot(a, b, preferred_element_type=F32)


def silu(v):
    half = 0.5 * v
    return half + half * jnp.tanh(half)


def norm_rows(values, gain):
    center = values - jnp.mean(values, axis=-1, keepdims=True)
    spread = jnp.mean(center * center, axis=-1, keepdims=True)
    return (center * lax.rsqrt(spread + 1e-05) * gain).astype(BF16)


def odd_device():
    return lax.rem(lax.axis_index("mesh"), 2)


def early_device():
    me, count = lax.axis_index("mesh"), lax.axis_size("mesh")
    return (me == 0) | ((lax.rem(me, 2) == 1) & (me != count - 1))


def pair_kernel(sides, blocks, cnt, tgt_hbm, src_hbm, obs, cpl, *refs):
    outs = refs[: len(sides)]
    tgt, src, listed, xbuf, cbuf, acc, isem, csem, xsem = refs[-9:]
    slots = xbuf.shape[0]
    odd = odd_device()
    rows_of = {"off": 2 * odd, "on": 2 - 2 * odd, "self": 1}
    lows = [rows_of[side[0]] * blocks + side[1] for side in sides]
    highs = [low + jnp.where(early_device(), side[2], side[4]) for low, side in zip(lows, sides)]
    sizes = [side[2] for side in sides]
    starts = [sum(sizes[:i]) for i in range(len(sizes))]
    reads = [
        pltpu.make_async_copy(tgt_hbm, tgt, isem.at[0]),
        pltpu.make_async_copy(src_hbm, src, isem.at[1]),
        pltpu.make_async_copy(cpl, cbuf, csem),
    ]
    for read in reads:
        read.start()
    reads[0].wait()
    reads[1].wait()
    groups = sum(sizes)

    def fetch(e, words):
        t = tgt[e]
        live, mine, group = e < cnt[0], jnp.bool_(False), jnp.int32(0)
        for low, high, start in zip(lows, highs, starts):
            here = live & (t >= low) & (t < high)
            mine = mine | here
            group = jnp.where(here, t - low + start, group)
        word = words[0]
        for i in range(1, len(words)):
            word = jnp.where(group >= 4 * i, words[i], word)
        shift = 8 * (group & 3)

        @pl.when(mine)
        def _():
            pltpu.make_async_copy(obs.at[src[e]], xbuf.at[e], xsem.at[e]).start()
            listed[group * slots + ((word >> shift) & 255)] = e

        return [
            word + jnp.where(mine & (group >= 4 * i) & (group < 4 * i + 4), 1 << shift, 0)
            for i, word in enumerate(words)
        ]

    words = lax.fori_loop(0, slots, fetch, [jnp.int32(0)] * pl.cdiv(groups, 4), unroll=8)
    reads[2].wait()

    for g in range(groups):
        number = (words[g // 4] >> (8 * (g % 4))) & 255
        def some(first, n):
            at = [listed[g * slots + first + i] for i in range(n)]
            for e in at:
                pltpu.make_async_copy(obs.at[0], xbuf.at[e], xsem.at[e]).wait()
            left = jnp.concatenate([cbuf[e] for e in at], axis=1)
            right = jnp.concatenate([xbuf[e] for e in at], axis=0)
            return dot(left, right)

        @pl.when(number % 4 == 0)
        def _():
            acc[...] = jnp.zeros_like(acc)

        for n in range(1, 4):

            @pl.when(number % 4 == n)
            def _():
                acc[...] = some(0, n)

        def four(j, carry):
            acc[...] += some(number % 4 + 4 * j, 4)
            return carry

        lax.fori_loop(0, number // 4, four, 0)

        side = max(i for i, start in enumerate(starts) if start <= g)
        outs[side][g - starts[side]] = acc[...].astype(outs[side].dtype)


def pair_sums(sides, blocks, tgt, src, cnt, obs, cpl, after=(), late_only=False):
    slots, rows, width = tgt.shape[0], obs.shape[1], obs.shape[2]
    more = list(after)

    def kernel(*refs):
        def run():
            pair_kernel(sides, blocks, *refs[:5], *refs[5 + len(more) :])

        if late_only:
            pl.when(jnp.logical_not(early_device()))(run)
        else:
            run()

    return pl.pallas_call(
        kernel,
        input_output_aliases={5: 0} if late_only else {},
        out_shape=[jax.ShapeDtypeStruct((side[2], rows, width), side[3]) for side in sides],
        in_specs=[SMEM] + [HBM] * 4 + [VMEM if late_only and i == 0 else pl.BlockSpec(memory_space=pl.ANY) for i in range(len(more))],
        out_specs=[VMEM] * len(sides),
        scratch_shapes=[
            pltpu.SMEM((slots,), jnp.int32),
            pltpu.SMEM((slots,), jnp.int32),
            pltpu.SMEM((sum(side[2] for side in sides) * slots,), jnp.int32),
            pltpu.VMEM((slots, rows, width), BF16),
            pltpu.VMEM((slots, rows, rows), BF16),
            pltpu.VMEM((rows, width), F32),
            pltpu.SemaphoreType.DMA((2,)),
            pltpu.SemaphoreType.DMA,
            pltpu.SemaphoreType.DMA((slots,)),
        ],
        compiler_params=pltpu.CompilerParams(vmem_limit_bytes=12 << 20),
        cost_estimate=pl.CostEstimate(flops=1 << 20, bytes_accessed=1 << 20, transcendentals=0),
        name="pairs_" + "_".join(side[0] for side in sides) + ("_late" if late_only else ""),
    )(cnt, *[pltpu.with_memory_space_constraint(x, pltpu.HBM) for x in (tgt, src, obs, cpl)], *more)


def call(kernel, out, arrays, name, scalars=(), late=(), weight=20, place=VMEM, scratch=()):
    return pl.pallas_call(
        kernel,
        out_shape=out,
        in_specs=[SMEM] * len(scalars) + [pl.BlockSpec(memory_space=pl.ANY)] * len(late) + [VMEM] * len(arrays),
        out_specs=[place] * len(out),
        scratch_shapes=list(scratch),
        compiler_params=pltpu.CompilerParams(vmem_limit_bytes=14 << 20),
        cost_estimate=pl.CostEstimate(flops=1 << weight, bytes_accessed=1 << 20, transcendentals=0),
        name=name,
    )(*scalars, *late, *arrays)


def read_rim(rim_ref, rim, sem):
    copy = pltpu.make_async_copy(rim_ref, rim, sem)
    copy.start()

    def get():
        copy.wait()
        odd = odd_device()
        return rim[0, odd], rim[0, 1 - odd]

    return get


RIM = (pltpu.SMEM((1, 2), jnp.int32), pltpu.SemaphoreType.DMA)


def updates(states, pres, incoming, w_in, w_out):
    first = [dot(x, w_in) for x in incoming]
    hidden = [silu(p + x).astype(BF16) for p, x in zip(pres, first)]
    second = [dot(x, w_out) for x in hidden]
    return [(s.astype(F32) + x).astype(BF16) for s, x in zip(states, second)]


def prepare_kernel(nbr, state, gain, w_self, coupling, pre, mix):
    blocks, rows = state.shape[0], state.shape[1]
    odd = odd_device()
    last = blocks + 1
    codes = [1 + c for c in range(blocks)] + [last * odd, last - last * odd]
    for m in range(blocks):
        pre[m] = dot(norm_rows(state[m].astype(F32), gain[...]), w_self[...])
        before, after, other = [coupling[m, k] for k in range(1, 4)]
        zero = jnp.zeros_like(other)
        for c, code in enumerate(codes):
            total = jnp.where(nbr[m, 3] == code, other, zero)
            if c == m:
                total = total + coupling[m, 0]
            if c < m or c >= blocks:
                total = total + jnp.where(nbr[m, 1] == code, before, zero)
            if c > m:
                total = total + jnp.where(nbr[m, 2] == code, after, zero)
            mix[m, :, c * rows : (c + 1) * rows] = total


def encode_kernel(first, pre, base, own, on, off, w_obs, w_out, gain, state, normed):
    number = off.shape[0]
    each = range(first, first + number)
    summed = [(own[m] + on[m].astype(F32) + off[m - first].astype(F32)).astype(BF16) for m in each]
    updated = updates([base[m] for m in each], [pre[m] for m in each], summed, w_obs[...], w_out[...])
    for i in range(number):
        state[i] = updated[i]
        normed[i] = norm_rows(updated[i].astype(F32), gain[:1, :])


def encode_rest_kernel(
    rim_ref, pre, base, own, on, off, w_obs, w_out, gain, state_a, normed_a, mix,
    state, normed, rim_on, rim_off, packed, row, rim, sem,
):
    blocks, rows, width = own.shape
    half = blocks - off.shape[0]
    rims = read_rim(rim_ref, rim, sem)
    state[:half] = state_a[...]
    normed[:half] = normed_a[...]
    tail = pl.ds(half, blocks - half)
    encode_kernel(half, pre, base, own, on, off, w_obs, w_out, gain, state.at[tail], normed.at[tail])
    off_rim, on_rim = rims()
    rim_on[...] = normed[on_rim]
    rim_off[...] = normed[off_rim]
    size = blocks * rows
    packed[:, :width] = state[off_rim]
    packed[:, width:] = mix[off_rim, :, size : size + rows]
    row[...] = mix[off_rim]


def part_kernel(row, normed, part):
    blocks, rows, width = normed.shape
    size = blocks * rows
    part[...] = dot(row[:, :size], normed[...].reshape(size, width))


def message_kernel(row, part, on, _, message):
    message[...] = (part[...] + dot(row[:, row.shape[1] - on.shape[0] :], on[...])).astype(BF16)


def neighbour_kernel(packed, rim_off, node_gain, n_self, _, state, normed, pre, message):
    rows, width = state.shape
    values = packed[:, :width]
    state[...] = values
    result = norm_rows(values.astype(F32), node_gain[:1, :])
    normed[...] = result
    pre[...] = dot(result, n_self[0])
    message[...] = dot(packed[:, width:], rim_off[...])


def round_kernel(rim_ref, mix, off, on, pre, heard, state, n_msg, n_out, gain, new_state, new_normed, rim_on, rim, sem):
    blocks, rows, width = state.shape
    rims = read_rim(rim_ref, rim, sem)
    size = blocks * rows
    sides = jnp.concatenate([off[...], on[...]], axis=0)
    each = range(blocks)
    incoming = [(heard[m] + dot(mix[m, :, size:], sides)).astype(BF16) for m in each]
    updated = updates([state[m] for m in each], [pre[m] for m in each], incoming, n_msg[0], n_out[0])
    for m in each:
        new_state[m] = updated[m]
        new_normed[m] = norm_rows(updated[m].astype(F32), gain[1:2, :])
    rim_on[...] = new_normed[rims()[1]]


def local_kernel(r, mix, normed, n_self, pre, message):
    blocks, rows, width = normed.shape
    size = blocks * rows
    own = normed[...].reshape(size, width)
    pre[...] = dot(own, n_self[r]).reshape(pre.shape)
    message[...] = dot(mix[...].reshape(size, -1)[:, :size], own).reshape(message.shape)


def far_kernel(arrived, far_message, pre, state, n_msg, n_out, gain, normed):
    incoming = (arrived[...].astype(F32) + far_message[...]).astype(BF16)
    (updated,) = updates([state[...]], [pre[...]], [incoming], n_msg[0], n_out[0])
    normed[...] = norm_rows(updated.astype(F32), gain[1:2, :])


def last_kernel(far, on, mix, pre, message, state, n_msg, n_out, out, stage, sems):
    blocks, rows, width = state.shape
    size = blocks * rows
    rims = jnp.concatenate([far[...], on[...]], axis=0)
    each = range(blocks)
    incoming = [(message[m] + dot(mix[m, :, size:], rims)).astype(BF16) for m in each]
    updated = updates([state[m] for m in each], [pre[m] for m in each], incoming, n_msg[1], n_out[1])
    copies = [pltpu.make_async_copy(stage.at[m], out.at[m], sems.at[m]) for m in each]
    for m in each:
        stage[m] = updated[m]
        copies[m].start()
    for copy in copies:
        copy.wait()


def shards(
    mesh_state,
    obs_latent,
    pair_coupling,
    pair_target,
    pair_source,
    pair_count,
    mesh_coupling,
    neighbor,
    rim_send,
    enc_gain,
    enc_self,
    enc_obs,
    enc_out,
    node_gain,
    node_self,
    node_msg,
    node_out,
):
    blocks, rows, width = mesh_state.shape
    size = blocks * rows
    count = lax.axis_size("mesh")
    on_route = [(i, i ^ 1) for i in range(count)]
    off_route = [(i, (i + 1) % count if i % 2 else (i - 1) % count) for i in range(count)]

    def swap_off(x):
        return lax.ppermute(x, "mesh", off_route)

    def swap_on(x):
        return lax.ppermute(x, "mesh", on_route)

    def shape(*dims, dtype=BF16):
        return jax.ShapeDtypeStruct(dims, dtype)

    whole, block = (blocks, rows, width), (rows, width)
    pairs = (pair_target, pair_source, pair_count, obs_latent, pair_coupling)
    half = blocks // 2
    rest = blocks - half
    sent, sent_rest = pair_sums([("off", 0, half, BF16, half), ("off", half, rest, BF16, 0)], blocks, *pairs)
    off_a = swap_off(sent)
    (sent,) = pair_sums([("off", half, rest, BF16, rest)], blocks, *pairs, after=(sent_rest, sent), late_only=True)
    off_b = swap_off(sent)
    sides = [("on", 0, blocks, BF16, blocks), ("self", 0, blocks, F32, blocks)]
    sent_on, sums_own = pair_sums(sides, blocks, *pairs, after=(sent,))
    sums_on = swap_on(sent_on)
    pre, mix = call(
        prepare_kernel,
        [shape(*whole, dtype=F32), shape(blocks, rows, size + 2 * rows)],
        [mesh_state, enc_gain[None], enc_self, mesh_coupling],
        "prepare",
        scalars=[neighbor],
        weight=34,
    )
    encode = [pre, mesh_state, sums_own, sums_on]
    weights = [enc_obs, enc_out, node_gain]
    halves = [shape(half, rows, width), shape(half, rows, width)]
    state, normed = call(
        lambda *refs: encode_kernel(0, *refs), halves, [*encode, off_a, *weights], "encode_first"
    )
    state, normed, rim_on, rim_off, packed, row = call(
        encode_rest_kernel,
        [
            shape(*whole),
            shape(*whole),
            shape(*block),
            shape(*block),
            shape(rows, width + rows),
            shape(rows, size + 2 * rows),
        ],
        [*encode, off_b, *weights, state, normed, mix],
        "encode_rest",
        late=[rim_send],
        scratch=RIM,
    )
    packed = swap_off(packed)
    on = swap_on(rim_on)
    (part,) = call(part_kernel, [shape(*block, dtype=F32)], [row, normed], "rim_part")
    pre, heard = call(
        lambda *refs: local_kernel(0, *refs),
        [shape(*whole, dtype=F32), shape(*whole, dtype=F32)],
        [mix, normed, node_self],
        "round_0_local",
    )
    (message,) = call(message_kernel, [shape(*block)], [row, part, on, heard], "rim_message")
    arrived = swap_off(message)
    far_state, far, far_pre, far_message = call(
        neighbour_kernel,
        [shape(*block), shape(*block), shape(*block, dtype=F32), shape(*block, dtype=F32)],
        [packed, rim_off, node_gain, node_self, message],
        "neighbour_rim",
    )
    state, normed, rim_on = call(
        round_kernel,
        [shape(*whole), shape(*whole), shape(*block)],
        [mix, far, on, pre, heard, state, node_msg, node_out, node_gain],
        "round_0",
        late=[rim_send],
        scratch=RIM,
    )
    on = swap_on(rim_on)
    pre, message = call(
        lambda *refs: local_kernel(1, *refs),
        [shape(*whole, dtype=F32), shape(*whole, dtype=F32)],
        [mix, normed, node_self],
        "round_1_local",
    )
    (far,) = call(
        far_kernel,
        [shape(*block)],
        [arrived, far_message, far_pre, far_state, node_msg, node_out, node_gain],
        "far_rim",
    )
    (out,) = call(
        last_kernel,
        [shape(*whole)],
        [far, on, mix, pre, message, state, node_msg, node_out],
        "round_1",
        place=HBM,
        scratch=[pltpu.VMEM(whole, BF16), pltpu.SemaphoreType.DMA((blocks,))],
    )
    return out


def solution(mesh):
    block = P(("groups", "mesh"), None, None)
    return jax.shard_map(
        shards,
        mesh=mesh,
        in_specs=(
            block,
            block,
            block,
            P(("groups", "mesh")),
            P(("groups", "mesh")),
            P(("groups", "mesh")),
            P("mesh", None, None, None),
            P("mesh", None),
            P("mesh", None),
        )
        + (P(),) * 8,
        out_specs=block,
        check_vma=False,
    )
```

```python
import jax
import jax.numpy as jnp
from jax import lax
from jax.experimental import pallas as pl
from jax.experimental.pallas import tpu as pltpu
from jax.sharding import PartitionSpec as P

F32 = jnp.float32
BF16 = jnp.bfloat16
VMEM = pl.BlockSpec(memory_space=pltpu.VMEM)
SMEM = pl.BlockSpec(memory_space=pltpu.SMEM)
HBM = pl.BlockSpec(memory_space=pltpu.HBM)


def dot(a, b):
    return jnp.dot(a, b, preferred_element_type=F32)


def silu(v):
    half = 0.5 * v
    return half + half * jnp.tanh(half)


def norm_rows(values, gain):
    center = values - jnp.mean(values, axis=-1, keepdims=True)
    spread = jnp.mean(center * center, axis=-1, keepdims=True)
    return (center * lax.rsqrt(spread + 1e-05) * gain).astype(BF16)


def odd_device():
    return lax.rem(lax.axis_index("mesh"), 2)


def early_device():
    me, count = lax.axis_index("mesh"), lax.axis_size("mesh")
    return (me == 0) | ((lax.rem(me, 2) == 1) & (me != count - 1))


def pair_kernel(sides, blocks, cnt, tgt_hbm, src_hbm, obs, cpl, *refs):
    outs = refs[: len(sides)]
    tgt, src, listed, xbuf, cbuf, acc, isem, csem, xsem = refs[-9:]
    slots = xbuf.shape[0]
    odd = odd_device()
    rows_of = {"off": 2 * odd, "on": 2 - 2 * odd, "self": 1}
    lows = [rows_of[side[0]] * blocks + side[1] for side in sides]
    highs = [low + jnp.where(early_device(), side[2], side[4]) for low, side in zip(lows, sides)]
    sizes = [side[2] for side in sides]
    starts = [sum(sizes[:i]) for i in range(len(sizes))]
    reads = [
        pltpu.make_async_copy(tgt_hbm, tgt, isem.at[0]),
        pltpu.make_async_copy(src_hbm, src, isem.at[1]),
        pltpu.make_async_copy(cpl, cbuf, csem),
    ]
    for read in reads:
        read.start()
    reads[0].wait()
    reads[1].wait()
    groups = sum(sizes)

    def fetch(e, words):
        t = tgt[e]
        live, mine, group = e < cnt[0], jnp.bool_(False), jnp.int32(0)
        for low, high, start in zip(lows, highs, starts):
            here = live & (t >= low) & (t < high)
            mine = mine | here
            group = jnp.where(here, t - low + start, group)
        word = words[0]
        for i in range(1, len(words)):
            word = jnp.where(group >= 4 * i, words[i], word)
        shift = 8 * (group & 3)

        @pl.when(mine)
        def _():
            pltpu.make_async_copy(obs.at[src[e]], xbuf.at[e], xsem.at[e]).start()
            listed[group * slots + ((word >> shift) & 255)] = e

        return [
            word + jnp.where(mine & (group >= 4 * i) & (group < 4 * i + 4), 1 << shift, 0)
            for i, word in enumerate(words)
        ]

    words = lax.fori_loop(0, slots, fetch, [jnp.int32(0)] * pl.cdiv(groups, 4), unroll=8)
    reads[2].wait()

    for g in range(groups):
        number = (words[g // 4] >> (8 * (g % 4))) & 255
        def some(first, n):
            at = [listed[g * slots + first + i] for i in range(n)]
            for e in at:
                pltpu.make_async_copy(obs.at[0], xbuf.at[e], xsem.at[e]).wait()
            left = jnp.concatenate([cbuf[e] for e in at], axis=1)
            right = jnp.concatenate([xbuf[e] for e in at], axis=0)
            return dot(left, right)

        @pl.when(number % 4 == 0)
        def _():
            acc[...] = jnp.zeros_like(acc)

        for n in range(1, 4):

            @pl.when(number % 4 == n)
            def _():
                acc[...] = some(0, n)

        def four(j, carry):
            acc[...] += some(number % 4 + 4 * j, 4)
            return carry

        lax.fori_loop(0, number // 4, four, 0)

        side = max(i for i, start in enumerate(starts) if start <= g)
        outs[side][g - starts[side]] = acc[...].astype(outs[side].dtype)


def pair_sums(sides, blocks, tgt, src, cnt, obs, cpl, after=(), late_only=False):
    slots, rows, width = tgt.shape[0], obs.shape[1], obs.shape[2]
    more = list(after)

    def kernel(*refs):
        def run():
            pair_kernel(sides, blocks, *refs[:5], *refs[5 + len(more) :])

        if late_only:
            pl.when(jnp.logical_not(early_device()))(run)
        else:
            run()

    return pl.pallas_call(
        kernel,
        input_output_aliases={5: 0} if late_only else {},
        out_shape=[jax.ShapeDtypeStruct((side[2], rows, width), side[3]) for side in sides],
        in_specs=[SMEM] + [HBM] * 4 + [VMEM if late_only and i == 0 else pl.BlockSpec(memory_space=pl.ANY) for i in range(len(more))],
        out_specs=[VMEM] * len(sides),
        scratch_shapes=[
            pltpu.SMEM((slots,), jnp.int32),
            pltpu.SMEM((slots,), jnp.int32),
            pltpu.SMEM((sum(side[2] for side in sides) * slots,), jnp.int32),
            pltpu.VMEM((slots, rows, width), BF16),
            pltpu.VMEM((slots, rows, rows), BF16),
            pltpu.VMEM((rows, width), F32),
            pltpu.SemaphoreType.DMA((2,)),
            pltpu.SemaphoreType.DMA,
            pltpu.SemaphoreType.DMA((slots,)),
        ],
        compiler_params=pltpu.CompilerParams(vmem_limit_bytes=12 << 20),
        cost_estimate=pl.CostEstimate(flops=1 << 20, bytes_accessed=1 << 20, transcendentals=0),
        name="pairs_" + "_".join(side[0] for side in sides) + ("_late" if late_only else ""),
    )(cnt, *[pltpu.with_memory_space_constraint(x, pltpu.HBM) for x in (tgt, src, obs, cpl)], *more)


def call(kernel, out, arrays, name, scalars=(), late=(), weight=20, place=VMEM, scratch=()):
    return pl.pallas_call(
        kernel,
        out_shape=out,
        in_specs=[SMEM] * len(scalars) + [pl.BlockSpec(memory_space=pl.ANY)] * len(late) + [VMEM] * len(arrays),
        out_specs=[place] * len(out),
        scratch_shapes=list(scratch),
        compiler_params=pltpu.CompilerParams(vmem_limit_bytes=14 << 20),
        cost_estimate=pl.CostEstimate(flops=1 << weight, bytes_accessed=1 << 20, transcendentals=0),
        name=name,
    )(*scalars, *late, *arrays)


def read_rim(rim_ref, rim, sem):
    copy = pltpu.make_async_copy(rim_ref, rim, sem)
    copy.start()

    def get():
        copy.wait()
        odd = odd_device()
        return rim[0, odd], rim[0, 1 - odd]

    return get


RIM = (pltpu.SMEM((1, 2), jnp.int32), pltpu.SemaphoreType.DMA)


def updates(states, pres, incoming, w_in, w_out):
    first = [dot(x, w_in) for x in incoming]
    hidden = [silu(p + x).astype(BF16) for p, x in zip(pres, first)]
    second = [dot(x, w_out) for x in hidden]
    return [(s.astype(F32) + x).astype(BF16) for s, x in zip(states, second)]


def prepare_kernel(nbr_ref, state, gain, w_self, coupling, pre, mix, nbr, sem):
    read = pltpu.make_async_copy(nbr_ref, nbr, sem)
    read.start()
    blocks, rows = state.shape[0], state.shape[1]
    odd = odd_device()
    last = blocks + 1
    codes = [1 + c for c in range(blocks)] + [last * odd, last - last * odd]
    normed = [norm_rows(state[m].astype(F32), gain[...]) for m in range(blocks)]
    for m in range(blocks):
        pre[m] = dot(normed[m], w_self[...])
    read.wait()
    for m in range(blocks):
        before, after, other = [coupling[m, k] for k in range(1, 4)]
        zero = jnp.zeros_like(other)
        for c, code in enumerate(codes):
            total = jnp.where(nbr[m, 3] == code, other, zero)
            if c == m:
                total = total + coupling[m, 0]
            if c < m or c >= blocks:
                total = total + jnp.where(nbr[m, 1] == code, before, zero)
            if c > m:
                total = total + jnp.where(nbr[m, 2] == code, after, zero)
            mix[m, :, c * rows : (c + 1) * rows] = total


def encode_kernel(first, pre, base, own, on, off, w_obs, w_out, gain, state, normed):
    number = off.shape[0]
    each = range(first, first + number)
    summed = [(own[m] + on[m].astype(F32) + off[m - first].astype(F32)).astype(BF16) for m in each]
    updated = updates([base[m] for m in each], [pre[m] for m in each], summed, w_obs[...], w_out[...])
    for i in range(number):
        state[i] = updated[i]
        normed[i] = norm_rows(updated[i].astype(F32), gain[:1, :])


def encode_rest_kernel(
    rim_ref, pre, base, own, on, off, w_obs, w_out, gain, state_a, normed_a, mix,
    state, normed, rim_on, rim_off, packed, row, rim, sem,
):
    blocks, rows, width = own.shape
    half = blocks - off.shape[0]
    rims = read_rim(rim_ref, rim, sem)
    state[:half] = state_a[...]
    normed[:half] = normed_a[...]
    tail = pl.ds(half, blocks - half)
    encode_kernel(half, pre, base, own, on, off, w_obs, w_out, gain, state.at[tail], normed.at[tail])
    off_rim, on_rim = rims()
    rim_on[...] = normed[on_rim]
    rim_off[...] = normed[off_rim]
    size = blocks * rows
    packed[:, :width] = state[off_rim]
    packed[:, width:] = mix[off_rim, :, size : size + rows]
    row[...] = mix[off_rim]


def part_kernel(row, normed, part):
    blocks, rows, width = normed.shape
    size = blocks * rows
    part[...] = dot(row[:, :size], normed[...].reshape(size, width))


def message_kernel(row, part, on, _, message):
    message[...] = (part[...] + dot(row[:, row.shape[1] - on.shape[0] :], on[...])).astype(BF16)


def neighbour_kernel(packed, rim_off, node_gain, n_self, _, state, normed, pre, message):
    rows, width = state.shape
    values = packed[:, :width]
    state[...] = values
    result = norm_rows(values.astype(F32), node_gain[:1, :])
    normed[...] = result
    pre[...] = dot(result, n_self[0])
    message[...] = dot(packed[:, width:], rim_off[...])


def round_kernel(rim_ref, mix, off, on, pre, heard, state, n_msg, n_out, gain, new_state, new_normed, rim_on, rim, sem):
    blocks, rows, width = state.shape
    rims = read_rim(rim_ref, rim, sem)
    size = blocks * rows
    sides = jnp.concatenate([off[...], on[...]], axis=0)
    each = range(blocks)
    incoming = [(heard[m] + dot(mix[m, :, size:], sides)).astype(BF16) for m in each]
    updated = updates([state[m] for m in each], [pre[m] for m in each], incoming, n_msg[0], n_out[0])
    for m in each:
        new_state[m] = updated[m]
        new_normed[m] = norm_rows(updated[m].astype(F32), gain[1:2, :])
    rim_on[...] = new_normed[rims()[1]]


def local_kernel(r, mix, normed, n_self, pre, message):
    blocks, rows, width = normed.shape
    size = blocks * rows
    own = normed[...].reshape(size, width)
    pre[...] = dot(own, n_self[r]).reshape(pre.shape)
    message[...] = dot(mix[...].reshape(size, -1)[:, :size], own).reshape(message.shape)


def far_kernel(arrived, far_message, pre, state, n_msg, n_out, gain, normed):
    incoming = (arrived[...].astype(F32) + far_message[...]).astype(BF16)
    (updated,) = updates([state[...]], [pre[...]], [incoming], n_msg[0], n_out[0])
    normed[...] = norm_rows(updated.astype(F32), gain[1:2, :])


def last_kernel(far, on, mix, pre, message, state, n_msg, n_out, out, stage, sems):
    blocks, rows, width = state.shape
    size = blocks * rows
    rims = jnp.concatenate([far[...], on[...]], axis=0)
    each = range(blocks)
    incoming = [(message[m] + dot(mix[m, :, size:], rims)).astype(BF16) for m in each]
    first = [dot(x, n_msg[1]) for x in incoming]
    hidden = [silu(pre[m] + first[m]).astype(BF16) for m in each]
    copies = [pltpu.make_async_copy(stage.at[m], out.at[m], sems.at[m]) for m in each]
    for m in each:
        stage[m] = (state[m].astype(F32) + dot(hidden[m], n_out[1])).astype(BF16)
        copies[m].start()
    for copy in copies:
        copy.wait()


def shards(
    mesh_state,
    obs_latent,
    pair_coupling,
    pair_target,
    pair_source,
    pair_count,
    mesh_coupling,
    neighbor,
    rim_send,
    enc_gain,
    enc_self,
    enc_obs,
    enc_out,
    node_gain,
    node_self,
    node_msg,
    node_out,
):
    blocks, rows, width = mesh_state.shape
    size = blocks * rows
    count = lax.axis_size("mesh")
    on_route = [(i, i ^ 1) for i in range(count)]
    off_route = [(i, (i + 1) % count if i % 2 else (i - 1) % count) for i in range(count)]

    def swap_off(x):
        return lax.ppermute(x, "mesh", off_route)

    def swap_on(x):
        return lax.ppermute(x, "mesh", on_route)

    def shape(*dims, dtype=BF16):
        return jax.ShapeDtypeStruct(dims, dtype)

    whole, block = (blocks, rows, width), (rows, width)
    pairs = (pair_target, pair_source, pair_count, obs_latent, pair_coupling)
    half = blocks // 2
    rest = blocks - half
    sent, sent_rest = pair_sums([("off", 0, half, BF16, half), ("off", half, rest, BF16, 0)], blocks, *pairs)
    off_a = swap_off(sent)
    (sent,) = pair_sums([("off", half, rest, BF16, rest)], blocks, *pairs, after=(sent_rest, sent), late_only=True)
    off_b = swap_off(sent)
    sides = [("on", 0, blocks, BF16, blocks), ("self", 0, blocks, F32, blocks)]
    sent_on, sums_own = pair_sums(sides, blocks, *pairs, after=(sent,))
    sums_on = swap_on(sent_on)
    pre, mix = call(
        prepare_kernel,
        [shape(*whole, dtype=F32), shape(blocks, rows, size + 2 * rows)],
        [mesh_state, enc_gain[None], enc_self, mesh_coupling],
        "prepare",
        late=[neighbor],
        scratch=(pltpu.SMEM(neighbor.shape, jnp.int32), pltpu.SemaphoreType.DMA),
        weight=34,
    )
    encode = [pre, mesh_state, sums_own, sums_on]
    weights = [enc_obs, enc_out, node_gain]
    halves = [shape(half, rows, width), shape(half, rows, width)]
    state, normed = call(
        lambda *refs: encode_kernel(0, *refs), halves, [*encode, off_a, *weights], "encode_first"
    )
    state, normed, rim_on, rim_off, packed, row = call(
        encode_rest_kernel,
        [
            shape(*whole),
            shape(*whole),
            shape(*block),
            shape(*block),
            shape(rows, width + rows),
            shape(rows, size + 2 * rows),
        ],
        [*encode, off_b, *weights, state, normed, mix],
        "encode_rest",
        late=[rim_send],
        scratch=RIM,
    )
    packed = swap_off(packed)
    on = swap_on(rim_on)
    (part,) = call(part_kernel, [shape(*block, dtype=F32)], [row, normed], "rim_part")
    pre, heard = call(
        lambda *refs: local_kernel(0, *refs),
        [shape(*whole, dtype=F32), shape(*whole, dtype=F32)],
        [mix, normed, node_self],
        "round_0_local",
    )
    (message,) = call(message_kernel, [shape(*block)], [row, part, on, heard], "rim_message")
    arrived = swap_off(message)
    far_state, far, far_pre, far_message = call(
        neighbour_kernel,
        [shape(*block), shape(*block), shape(*block, dtype=F32), shape(*block, dtype=F32)],
        [packed, rim_off, node_gain, node_self, message],
        "neighbour_rim",
    )
    state, normed, rim_on = call(
        round_kernel,
        [shape(*whole), shape(*whole), shape(*block)],
        [mix, far, on, pre, heard, state, node_msg, node_out, node_gain],
        "round_0",
        late=[rim_send],
        scratch=RIM,
    )
    on = swap_on(rim_on)
    pre, message = call(
        lambda *refs: local_kernel(1, *refs),
        [shape(*whole, dtype=F32), shape(*whole, dtype=F32)],
        [mix, normed, node_self],
        "round_1_local",
    )
    (far,) = call(
        far_kernel,
        [shape(*block)],
        [arrived, far_message, far_pre, far_state, node_msg, node_out, node_gain],
        "far_rim",
    )
    (out,) = call(
        last_kernel,
        [shape(*whole)],
        [far, on, mix, pre, message, state, node_msg, node_out],
        "round_1",
        place=HBM,
        scratch=[pltpu.VMEM(whole, BF16), pltpu.SemaphoreType.DMA((blocks,))],
    )
    return out


def solution(mesh):
    block = P(("groups", "mesh"), None, None)
    return jax.shard_map(
        shards,
        mesh=mesh,
        in_specs=(
            block,
            block,
            block,
            P(("groups", "mesh")),
            P(("groups", "mesh")),
            P(("groups", "mesh")),
            P("mesh", None, None, None),
            P("mesh", None),
            P("mesh", None),
        )
        + (P(),) * 8,
        out_specs=block,
        check_vma=False,
    )
```

```python
import jax
import jax.numpy as jnp
from jax import lax
from jax.experimental import pallas as pl
from jax.experimental.pallas import tpu as pltpu
from jax.sharding import PartitionSpec as P

F32 = jnp.float32
BF16 = jnp.bfloat16
VMEM = pl.BlockSpec(memory_space=pltpu.VMEM)
SMEM = pl.BlockSpec(memory_space=pltpu.SMEM)
HBM = pl.BlockSpec(memory_space=pltpu.HBM)


def dot(a, b):
    return jnp.dot(a, b, preferred_element_type=F32)


def silu(v):
    half = 0.5 * v
    return half + half * jnp.tanh(half)


def norm_rows(values, gain):
    center = values - jnp.mean(values, axis=-1, keepdims=True)
    spread = jnp.mean(center * center, axis=-1, keepdims=True)
    return (center * lax.rsqrt(spread + 1e-05) * gain).astype(BF16)


def odd_device():
    return lax.rem(lax.axis_index("mesh"), 2)


def early_device():
    me, count = lax.axis_index("mesh"), lax.axis_size("mesh")
    return (me == 0) | ((lax.rem(me, 2) == 1) & (me != count - 1))


def pair_kernel(sides, blocks, cnt, tgt_hbm, src_hbm, obs, cpl, *refs):
    outs = refs[: len(sides)]
    tgt, src, listed, xbuf, cbuf, acc, isem, csem, xsem = refs[-9:]
    slots = xbuf.shape[0]
    odd = odd_device()
    rows_of = {"off": 2 * odd, "on": 2 - 2 * odd, "self": 1}
    lows = [rows_of[side[0]] * blocks + side[1] for side in sides]
    highs = [low + jnp.where(early_device(), side[2], side[4]) for low, side in zip(lows, sides)]
    sizes = [side[2] for side in sides]
    starts = [sum(sizes[:i]) for i in range(len(sizes))]
    reads = [
        pltpu.make_async_copy(tgt_hbm, tgt, isem.at[0]),
        pltpu.make_async_copy(src_hbm, src, isem.at[1]),
        pltpu.make_async_copy(cpl, cbuf, csem),
    ]
    for read in reads:
        read.start()
    reads[0].wait()
    reads[1].wait()
    groups = sum(sizes)

    def fetch(e, words):
        t = tgt[e]
        live, mine, group = e < cnt[0], jnp.bool_(False), jnp.int32(0)
        for low, high, start in zip(lows, highs, starts):
            here = live & (t >= low) & (t < high)
            mine = mine | here
            group = jnp.where(here, t - low + start, group)
        word = words[0]
        for i in range(1, len(words)):
            word = jnp.where(group >= 4 * i, words[i], word)
        shift = 8 * (group & 3)

        @pl.when(mine)
        def _():
            pltpu.make_async_copy(obs.at[src[e]], xbuf.at[e], xsem.at[e]).start()
            listed[group * slots + ((word >> shift) & 255)] = e

        return [
            word + jnp.where(mine & (group >= 4 * i) & (group < 4 * i + 4), 1 << shift, 0)
            for i, word in enumerate(words)
        ]

    words = lax.fori_loop(0, slots, fetch, [jnp.int32(0)] * pl.cdiv(groups, 4), unroll=8)
    reads[2].wait()

    for g in range(groups):
        number = (words[g // 4] >> (8 * (g % 4))) & 255
        def some(first, n):
            at = [listed[g * slots + first + i] for i in range(n)]
            for e in at:
                pltpu.make_async_copy(obs.at[0], xbuf.at[e], xsem.at[e]).wait()
            left = jnp.concatenate([cbuf[e] for e in at], axis=1)
            right = jnp.concatenate([xbuf[e] for e in at], axis=0)
            return dot(left, right)

        @pl.when(number % 4 == 0)
        def _():
            acc[...] = jnp.zeros_like(acc)

        for n in range(1, 4):

            @pl.when(number % 4 == n)
            def _():
                acc[...] = some(0, n)

        def four(j, carry):
            acc[...] += some(number % 4 + 4 * j, 4)
            return carry

        lax.fori_loop(0, number // 4, four, 0)

        side = max(i for i, start in enumerate(starts) if start <= g)
        outs[side][g - starts[side]] = acc[...].astype(outs[side].dtype)


def pair_sums(sides, blocks, tgt, src, cnt, obs, cpl, after=(), late_only=False):
    slots, rows, width = tgt.shape[0], obs.shape[1], obs.shape[2]
    more = list(after)

    def kernel(*refs):
        def run():
            pair_kernel(sides, blocks, *refs[:5], *refs[5 + len(more) :])

        if late_only:
            pl.when(jnp.logical_not(early_device()))(run)
        else:
            run()

    return pl.pallas_call(
        kernel,
        input_output_aliases={5: 0} if late_only else {},
        out_shape=[jax.ShapeDtypeStruct((side[2], rows, width), side[3]) for side in sides],
        in_specs=[SMEM] + [HBM] * 4 + [VMEM if late_only and i == 0 else pl.BlockSpec(memory_space=pl.ANY) for i in range(len(more))],
        out_specs=[VMEM] * len(sides),
        scratch_shapes=[
            pltpu.SMEM((slots,), jnp.int32),
            pltpu.SMEM((slots,), jnp.int32),
            pltpu.SMEM((sum(side[2] for side in sides) * slots,), jnp.int32),
            pltpu.VMEM((slots, rows, width), BF16),
            pltpu.VMEM((slots, rows, rows), BF16),
            pltpu.VMEM((rows, width), F32),
            pltpu.SemaphoreType.DMA((2,)),
            pltpu.SemaphoreType.DMA,
            pltpu.SemaphoreType.DMA((slots,)),
        ],
        compiler_params=pltpu.CompilerParams(vmem_limit_bytes=12 << 20),
        cost_estimate=pl.CostEstimate(flops=1 << 20, bytes_accessed=1 << 20, transcendentals=0),
        name="pairs_" + "_".join(side[0] for side in sides) + ("_late" if late_only else ""),
    )(cnt, *[pltpu.with_memory_space_constraint(x, pltpu.HBM) for x in (tgt, src, obs, cpl)], *more)


def call(kernel, out, arrays, name, scalars=(), late=(), weight=20, place=VMEM, scratch=()):
    return pl.pallas_call(
        kernel,
        out_shape=out,
        in_specs=[SMEM] * len(scalars) + [pl.BlockSpec(memory_space=pl.ANY)] * len(late) + [VMEM] * len(arrays),
        out_specs=[place] * len(out),
        scratch_shapes=list(scratch),
        compiler_params=pltpu.CompilerParams(vmem_limit_bytes=14 << 20),
        cost_estimate=pl.CostEstimate(flops=1 << weight, bytes_accessed=1 << 20, transcendentals=0),
        name=name,
    )(*scalars, *late, *arrays)


def read_rim(rim_ref, rim, sem):
    copy = pltpu.make_async_copy(rim_ref, rim, sem)
    copy.start()

    def get():
        copy.wait()
        odd = odd_device()
        return rim[0, odd], rim[0, 1 - odd]

    return get


RIM = (pltpu.SMEM((1, 2), jnp.int32), pltpu.SemaphoreType.DMA)


def updates(states, pres, incoming, w_in, w_out):
    first = [dot(x, w_in) for x in incoming]
    hidden = [silu(p + x).astype(BF16) for p, x in zip(pres, first)]
    second = [dot(x, w_out) for x in hidden]
    return [(s.astype(F32) + x).astype(BF16) for s, x in zip(states, second)]


def prepare_kernel(nbr, state, gain, w_self, coupling, pre, mix):
    blocks, rows = state.shape[0], state.shape[1]
    odd = odd_device()
    last = blocks + 1
    codes = [1 + c for c in range(blocks)] + [last * odd, last - last * odd]
    for m in range(blocks):
        pre[m] = dot(norm_rows(state[m].astype(F32), gain[...]), w_self[...])
        before, after, other = [coupling[m, k] for k in range(1, 4)]
        zero = jnp.zeros_like(other)
        for c, code in enumerate(codes):
            total = jnp.where(nbr[m, 3] == code, other, zero)
            if c == m:
                total = total + coupling[m, 0]
            if c < m or c >= blocks:
                total = total + jnp.where(nbr[m, 1] == code, before, zero)
            if c > m:
                total = total + jnp.where(nbr[m, 2] == code, after, zero)
            mix[m, :, c * rows : (c + 1) * rows] = total


def encode_kernel(first, pre, base, own, on, off, w_obs, w_out, gain, state, normed):
    number = off.shape[0]
    each = range(first, first + number)
    summed = [(own[m] + on[m].astype(F32) + off[m - first].astype(F32)).astype(BF16) for m in each]
    updated = updates([base[m] for m in each], [pre[m] for m in each], summed, w_obs[...], w_out[...])
    for i in range(number):
        state[i] = updated[i]
        normed[i] = norm_rows(updated[i].astype(F32), gain[:1, :])


def encode_rest_kernel(
    rim_ref, pre, base, own, on, off, w_obs, w_out, gain, state_a, normed_a, mix,
    state, normed, rim_on, rim_off, packed, row, rim, sem,
):
    blocks, rows, width = own.shape
    half = blocks - off.shape[0]
    rims = read_rim(rim_ref, rim, sem)
    state[:half] = state_a[...]
    normed[:half] = normed_a[...]
    tail = pl.ds(half, blocks - half)
    encode_kernel(half, pre, base, own, on, off, w_obs, w_out, gain, state.at[tail], normed.at[tail])
    off_rim, on_rim = rims()
    rim_on[...] = normed[on_rim]
    rim_off[...] = normed[off_rim]
    size = blocks * rows
    packed[:, :width] = state[off_rim]
    packed[:, width:] = mix[off_rim, :, size : size + rows]
    row[...] = mix[off_rim]


def part_kernel(row, normed, part):
    blocks, rows, width = normed.shape
    size = blocks * rows
    part[...] = dot(row[:, :size], normed[...].reshape(size, width))


def message_kernel(row, part, on, _, message):
    message[...] = (part[...] + dot(row[:, row.shape[1] - on.shape[0] :], on[...])).astype(BF16)


def neighbour_kernel(packed, node_gain, _, state, normed):
    values = packed[:, : state.shape[1]]
    state[...] = values
    normed[...] = norm_rows(values.astype(F32), node_gain[:1, :])


def far_part_kernel(packed, rim_off, far, n_self, _, pre, message):
    pre[...] = dot(far[...], n_self[0])
    message[...] = dot(packed[:, far.shape[1] :], rim_off[...])


def round_kernel(rim_ref, mix, off, on, pre, heard, state, n_msg, n_out, gain, new_state, new_normed, rim_on, rim, sem):
    blocks, rows, width = state.shape
    rims = read_rim(rim_ref, rim, sem)
    size = blocks * rows
    sides = jnp.concatenate([off[...], on[...]], axis=0)
    each = range(blocks)
    incoming = [(heard[m] + dot(mix[m, :, size:], sides)).astype(BF16) for m in each]
    updated = updates([state[m] for m in each], [pre[m] for m in each], incoming, n_msg[0], n_out[0])
    for m in each:
        new_state[m] = updated[m]
        new_normed[m] = norm_rows(updated[m].astype(F32), gain[1:2, :])
    rim_on[...] = new_normed[rims()[1]]


def local_kernel(r, mix, normed, n_self, pre, message):
    blocks, rows, width = normed.shape
    size = blocks * rows
    own = normed[...].reshape(size, width)
    pre[...] = dot(own, n_self[r]).reshape(pre.shape)
    message[...] = dot(mix[...].reshape(size, -1)[:, :size], own).reshape(message.shape)


def far_kernel(arrived, far_message, pre, state, n_msg, n_out, gain, normed):
    incoming = (arrived[...].astype(F32) + far_message[...]).astype(BF16)
    (updated,) = updates([state[...]], [pre[...]], [incoming], n_msg[0], n_out[0])
    normed[...] = norm_rows(updated.astype(F32), gain[1:2, :])


def last_kernel(far, on, mix, pre, message, state, n_msg, n_out, out, stage, sems):
    blocks, rows, width = state.shape
    size = blocks * rows
    rims = jnp.concatenate([far[...], on[...]], axis=0)
    each = range(blocks)
    incoming = [(message[m] + dot(mix[m, :, size:], rims)).astype(BF16) for m in each]
    updated = updates([state[m] for m in each], [pre[m] for m in each], incoming, n_msg[1], n_out[1])
    copies = [pltpu.make_async_copy(stage.at[m], out.at[m], sems.at[m]) for m in each]
    for m in each:
        stage[m] = updated[m]
        copies[m].start()
    for copy in copies:
        copy.wait()


def shards(
    mesh_state,
    obs_latent,
    pair_coupling,
    pair_target,
    pair_source,
    pair_count,
    mesh_coupling,
    neighbor,
    rim_send,
    enc_gain,
    enc_self,
    enc_obs,
    enc_out,
    node_gain,
    node_self,
    node_msg,
    node_out,
):
    blocks, rows, width = mesh_state.shape
    size = blocks * rows
    count = lax.axis_size("mesh")
    on_route = [(i, i ^ 1) for i in range(count)]
    off_route = [(i, (i + 1) % count if i % 2 else (i - 1) % count) for i in range(count)]

    def swap_off(x):
        return lax.ppermute(x, "mesh", off_route)

    def swap_on(x):
        return lax.ppermute(x, "mesh", on_route)

    def shape(*dims, dtype=BF16):
        return jax.ShapeDtypeStruct(dims, dtype)

    whole, block = (blocks, rows, width), (rows, width)
    pairs = (pair_target, pair_source, pair_count, obs_latent, pair_coupling)
    half = blocks // 2
    rest = blocks - half
    sent, sent_rest = pair_sums([("off", 0, half, BF16, half), ("off", half, rest, BF16, 0)], blocks, *pairs)
    off_a = swap_off(sent)
    (sent,) = pair_sums([("off", half, rest, BF16, rest)], blocks, *pairs, after=(sent_rest, sent), late_only=True)
    off_b = swap_off(sent)
    sides = [("on", 0, blocks, BF16, blocks), ("self", 0, blocks, F32, blocks)]
    sent_on, sums_own = pair_sums(sides, blocks, *pairs, after=(sent,))
    sums_on = swap_on(sent_on)
    pre, mix = call(
        prepare_kernel,
        [shape(*whole, dtype=F32), shape(blocks, rows, size + 2 * rows)],
        [mesh_state, enc_gain[None], enc_self, mesh_coupling],
        "prepare",
        scalars=[neighbor],
        weight=34,
    )
    encode = [pre, mesh_state, sums_own, sums_on]
    weights = [enc_obs, enc_out, node_gain]
    halves = [shape(half, rows, width), shape(half, rows, width)]
    state, normed = call(
        lambda *refs: encode_kernel(0, *refs), halves, [*encode, off_a, *weights], "encode_first"
    )
    state, normed, rim_on, rim_off, packed, row = call(
        encode_rest_kernel,
        [
            shape(*whole),
            shape(*whole),
            shape(*block),
            shape(*block),
            shape(rows, width + rows),
            shape(rows, size + 2 * rows),
        ],
        [*encode, off_b, *weights, state, normed, mix],
        "encode_rest",
        late=[rim_send],
        scratch=RIM,
    )
    packed = swap_off(packed)
    on = swap_on(rim_on)
    (part,) = call(part_kernel, [shape(*block, dtype=F32)], [row, normed], "rim_part")
    pre, heard = call(
        lambda *refs: local_kernel(0, *refs),
        [shape(*whole, dtype=F32), shape(*whole, dtype=F32)],
        [mix, normed, node_self],
        "round_0_local",
    )
    (message,) = call(message_kernel, [shape(*block)], [row, part, on, heard], "rim_message")
    arrived = swap_off(message)
    far_state, far = call(
        neighbour_kernel,
        [shape(*block), shape(*block)],
        [packed, node_gain, message],
        "neighbour_rim",
    )
    state, normed, rim_on = call(
        round_kernel,
        [shape(*whole), shape(*whole), shape(*block)],
        [mix, far, on, pre, heard, state, node_msg, node_out, node_gain],
        "round_0",
        late=[rim_send],
        scratch=RIM,
    )
    on = swap_on(rim_on)
    pre, message = call(
        lambda *refs: local_kernel(1, *refs),
        [shape(*whole, dtype=F32), shape(*whole, dtype=F32)],
        [mix, normed, node_self],
        "round_1_local",
    )
    far_pre, far_message = call(
        far_part_kernel,
        [shape(*block, dtype=F32), shape(*block, dtype=F32)],
        [packed, rim_off, far, node_self, rim_on],
        "far_part",
    )
    (far,) = call(
        far_kernel,
        [shape(*block)],
        [arrived, far_message, far_pre, far_state, node_msg, node_out, node_gain],
        "far_rim",
    )
    (out,) = call(
        last_kernel,
        [shape(*whole)],
        [far, on, mix, pre, message, state, node_msg, node_out],
        "round_1",
        place=HBM,
        scratch=[pltpu.VMEM(whole, BF16), pltpu.SemaphoreType.DMA((blocks,))],
    )
    return out


def solution(mesh):
    block = P(("groups", "mesh"), None, None)
    return jax.shard_map(
        shards,
        mesh=mesh,
        in_specs=(
            block,
            block,
            block,
            P(("groups", "mesh")),
            P(("groups", "mesh")),
            P(("groups", "mesh")),
            P("mesh", None, None, None),
            P("mesh", None),
            P("mesh", None),
        )
        + (P(),) * 8,
        out_specs=block,
        check_vma=False,
    )
```
